128 devices in a mesh: rep: 8 (over z, x_lo), tp: 16 (over y, x_hi, core).
Axes of the slice: x: 4 (x_hi: 2, x_lo: 2; x = x_hi * 2 + x_lo), y: 4, z: 4, core: 2. Of those that a mesh axis runs over, the one named last changes fastest.
Arguments:
- tokens: bfloat16 [1024, 4, 8192], P('rep', None, 'tp'), may hold values from -6 to 6
- query_weight_matrix: bfloat16 [8192, 8192], P(None, 'tp'), may hold values from -0.0625 to 0.0625
- key_value_weight: bfloat16 [8192, 2048], P(None, 'tp'), may hold values from -0.0625 to 0.0625
- adapter_down_factors: bfloat16 [64, 8192, 128], P('rep', 'tp'), may hold values from -0.0625 to 0.0625
- adapter_up_query: bfloat16 [64, 64, 8192], P('rep', None, 'tp'), may hold values from -0.375 to 0.375
- adapter_up_key_value: bfloat16 [64, 64, 2048], P('rep', None, 'tp'), may hold values from -0.375 to 0.375
- storage_slot_adapter: int32 [64], replicated, may hold values from 0 to 63, as said below
- slot_request_adapter: int32 [1024], replicated, may hold values from 0 to 63, as said below
- migration: int32 [1024], replicated, may hold values from 0 to 1023, as said below
- lengths: int32 [1024], P('rep'), may hold values from 1 to 124
- previous_block_table: int32 [1024, 8], P('rep'), may hold values from 0 to 1023, as said below
- moved_block_table: int32 [1024, 8], P('rep'), may hold values from 0 to 1023, as said below
- paged_cache_pool: bfloat16 [8192, 16, 2048], P('rep', None, 'tp'), may hold values from -900 to 900
Outputs:
- attention: bfloat16 [1024, 4, 8192], P('rep', None, 'tp')
- new_pool: bfloat16 [8192, 16, 2048], P('rep', None, 'tp')
The draws below stay inside these ranges and needn't reach their ends.
Inputs may be any that keep to these rules, and one draw needn't show every extreme that they name: `storage_slot_adapter`: a permutation of all adapters. `slot_request_adapter`: the requests in the new slots of one group name exactly 8 distinct adapters, and at most one of them is stored (slots g * 8 to g * 8 + 7 of storage_slot_adapter for group g) in any one other group. `migration`: a permutation of all requests; at most 8 requests move from one group to any one other group. `previous_block_table`: the rows of the 128 requests of one group name every block 0 to 1023 exactly once. `moved_block_table`: the rows of the 128 new slots of one group name every block 0 to 1023 exactly once.
All inputs are finite; a program needn't handle non-finite values.
Results may differ from the reference program's by a relative error of at most 0.018.
The reference program's roundings to bfloat16 on the way count: a program that leaves them out, or rounds other values in their place, can miss the bound.
Values may be sent and summed in bfloat16 or wider, within the bound.
No kernel may reach another device: no remote copies, remote signals or barrier semaphores. Data moves between devices by JAX's collectives and lax.ppermute only.
A program may use at most 128 MiB of HBM per device.

```python
import math
import jax
import jax.numpy as jnp
from jax import lax

MODEL_WIDTH = 8192
QUERY_HEADS = 64
KEY_VALUE_HEADS = 8
HEAD_SIZE = 128
ADAPTER_RANK = 64
STEPS = 4
PAGE = 16
MAXB = 8
ADP_DEV = 8
RQ_DEV = 128
REQUESTS = 1024
ADAPTER_COUNT = 64
POOL = 1024
LCAP = 128


def adapter_plan(key):
    group_count = ADAPTER_COUNT // ADP_DEV
    storage_slot_adapter = jax.random.permutation(jax.random.fold_in(key, 101), ADAPTER_COUNT).astype(jnp.int32)
    offsets = 1 + jax.random.permutation(jax.random.fold_in(key, 102), group_count - 1)
    kind_index = jnp.arange(ADP_DEV)
    remote = (kind_index >= 1) & (kind_index < group_count)
    shift_by = jnp.where(remote, offsets[jnp.clip(kind_index - 1, 0, group_count - 2)], 0)
    owners = (jnp.arange(group_count)[:, None] + shift_by[None, :]) % group_count
    usable = storage_slot_adapter[owners * ADP_DEV + kind_index[None, :]]
    picks_one = jax.random.randint(jax.random.fold_in(key, 103), (group_count, RQ_DEV), 0, ADP_DEV)
    picks_two = jax.random.randint(jax.random.fold_in(key, 104), (group_count, RQ_DEV), 0, ADP_DEV)
    row_index = jnp.arange(RQ_DEV)[None, :]
    pick_kind = jnp.where(row_index < ADP_DEV, row_index, ADP_DEV - 1 - jnp.minimum(picks_one, picks_two))
    shuffles = jax.vmap(lambda member: jax.random.permutation(member, RQ_DEV))(jax.random.split(jax.random.fold_in(key, 105), group_count))
    shuffled = jnp.take_along_axis(pick_kind, shuffles, axis=1)
    slot_request_adapter = jnp.take_along_axis(usable, shuffled, axis=1).reshape(REQUESTS).astype(jnp.int32)
    return (storage_slot_adapter, slot_request_adapter)


def draw_storage_slot_adapter(key, part):
    plan = adapter_plan(key)
    return plan[0]


def draw_slot_request_adapter(key, part):
    plan = adapter_plan(key)
    return plan[1]


def draw_migration(key, part):
    key = jax.random.fold_in(key, 41)
    group_count = REQUESTS // RQ_DEV
    capacity = RQ_DEV // (2 * group_count)
    counts = jax.random.randint(jax.random.fold_in(key, 1), (group_count - 1,), (capacity + 1) // 2, capacity + 1)
    counts = counts.at[jax.random.randint(jax.random.fold_in(key, 2), (), 0, group_count - 1)].set(capacity)
    ends = jnp.cumsum(counts)
    place = jnp.arange(RQ_DEV)
    offset_at = 1 + jnp.sum(place[:, None] >= ends[None, :], axis=1)
    offset_at = jnp.where(offset_at == group_count, 0, offset_at)
    orders = jax.vmap(lambda member: jax.random.permutation(member, RQ_DEV))(jax.random.split(jax.random.fold_in(key, 3), group_count))
    orders = orders + jnp.arange(group_count)[:, None] * RQ_DEV
    sources = (jnp.arange(group_count)[:, None] - offset_at[None, :]) % group_count
    before = orders[sources, place[None, :]]
    shuffles = jax.vmap(lambda member: jax.random.permutation(member, RQ_DEV))(jax.random.split(jax.random.fold_in(key, 4), group_count))
    return jnp.take_along_axis(before, shuffles, axis=1).reshape(REQUESTS).astype(jnp.int32)


def draw_lengths(key, part):
    key = jax.random.fold_in(key, 43)
    most = MAXB * PAGE - STEPS
    drawn = jax.random.randint(jax.random.fold_in(key, 1), (REQUESTS,), 1, most + 1)
    spot = jax.random.randint(jax.random.fold_in(key, 2), (), 0, REQUESTS)
    return drawn.at[spot].set(most).astype(jnp.int32)


def table_law(key):
    group_count = REQUESTS // RQ_DEV
    blocks = jax.vmap(lambda member: jax.random.permutation(member, RQ_DEV * MAXB))(jax.random.split(key, group_count))
    return blocks.reshape(REQUESTS, MAXB).astype(jnp.int32)


def draw_previous_block_table(key, part):
    key = jax.random.fold_in(key, 45)
    return table_law(key)


def draw_moved_block_table(key, part):
    key = jax.random.fold_in(key, 47)
    return table_law(key)


def draw_paged_cache_pool(key, part):
    key = jax.random.fold_in(key, 51)
    block_count = REQUESTS * MAXB
    breadth = 2 * KEY_VALUE_HEADS * HEAD_SIZE
    noise = jax.random.normal(jax.random.fold_in(key, 1), (block_count, PAGE, breadth), jnp.float32)
    pooled = noise
    return jnp.clip(pooled, -900.0, 900.0).astype(jnp.bfloat16)


def level_of(key, shape, shards, low, high):
    gain, own = 1.0, jax.random.fold_in(key, 6)
    for position, blocks in shards:
        draws = jnp.exp(jax.random.uniform(jax.random.fold_in(own, position), (blocks,), jnp.float32, low / len(shards), high / len(shards)))
        gain = gain * jnp.repeat(draws, shape[position] // blocks).reshape([-1 if axis == position else 1 for axis in range(len(shape))])
    return gain


def bell_draw(key, dims, scale, bound, cuts=(), kind=jnp.bfloat16):
    entries = jax.random.normal(key, dims, jnp.float32) * scale
    if len(cuts) > 0:
        entries = level_of(key, dims, cuts, -0.22, 0.18) * entries
    return jnp.clip(entries, min=-bound, max=bound).astype(kind)


def setup_inputs(seed: int = 0) -> dict:
    streams_of = jax.random.split(jax.random.key(seed), 14)
    return {
        "tokens": bell_draw(streams_of[0], (REQUESTS, STEPS, MODEL_WIDTH), 1.0, 6.0, ((0, 8), (2, 16))),
        "query_weight_matrix": bell_draw(streams_of[1], (MODEL_WIDTH, QUERY_HEADS * HEAD_SIZE), MODEL_WIDTH ** -0.5, 0.0625, ((1, 16),)),
        "key_value_weight": bell_draw(streams_of[2], (MODEL_WIDTH, 2 * KEY_VALUE_HEADS * HEAD_SIZE), MODEL_WIDTH ** -0.5, 0.0625, ((1, 16),)),
        "adapter_down_factors": bell_draw(streams_of[3], (ADAPTER_COUNT, MODEL_WIDTH, 2 * ADAPTER_RANK), MODEL_WIDTH ** -0.5, 0.0625, ((0, 8), (1, 16))),
        "adapter_up_query": bell_draw(streams_of[4], (ADAPTER_COUNT, ADAPTER_RANK, QUERY_HEADS * HEAD_SIZE), (4 * ADAPTER_RANK) ** -0.5, 0.375, ((0, 8), (2, 16))),
        "adapter_up_key_value": bell_draw(streams_of[5], (ADAPTER_COUNT, ADAPTER_RANK, 2 * KEY_VALUE_HEADS * HEAD_SIZE), (4 * ADAPTER_RANK) ** -0.5, 0.375, ((0, 8), (2, 16))),
        "storage_slot_adapter": draw_storage_slot_adapter(jax.random.fold_in(streams_of[13], 71), 0),
        "slot_request_adapter": draw_slot_request_adapter(jax.random.fold_in(streams_of[13], 71), 0),
        "migration": draw_migration(jax.random.fold_in(streams_of[13], 71), 0),
        "lengths": draw_lengths(jax.random.fold_in(streams_of[13], 71), 0),
        "previous_block_table": draw_previous_block_table(jax.random.fold_in(streams_of[13], 71), 0),
        "moved_block_table": draw_moved_block_table(jax.random.fold_in(streams_of[13], 71), 0),
        "paged_cache_pool": draw_paged_cache_pool(jax.random.fold_in(streams_of[13], 71), 0),
    }


THETA = 500000.0

def rotate(values, positions):
    head_width = values.shape[-1]
    half_width = head_width // 2
    frequency = THETA ** (-(jnp.arange(half_width, dtype=jnp.float32) * 2.0 / head_width))
    angles = positions.astype(jnp.float32)[..., None] * frequency
    cosine = jnp.cos(angles)
    sine_part = jnp.sin(angles)
    lower_half = values[..., :half_width]
    upper_half = values[..., half_width:]
    return jnp.concatenate([lower_half * cosine - upper_half * sine_part, upper_half * cosine + lower_half * sine_part], axis=-1)

def reference(tokens, query_weight_matrix, key_value_weight, adapter_down_factors, adapter_up_query, adapter_up_key_value, storage_slot_adapter, slot_request_adapter, migration, lengths, previous_block_table, moved_block_table, paged_cache_pool):
    moved = tokens[migration]
    flat_tokens = moved.reshape(REQUESTS * STEPS, MODEL_WIDTH)
    base_q = jnp.dot(flat_tokens, query_weight_matrix, preferred_element_type=jnp.float32).reshape(REQUESTS, STEPS, QUERY_HEADS * HEAD_SIZE)
    base_kv = jnp.dot(flat_tokens, key_value_weight, preferred_element_type=jnp.float32).reshape(REQUESTS, STEPS, 2 * KEY_VALUE_HEADS * HEAD_SIZE)
    storage = jnp.zeros((ADAPTER_COUNT,), jnp.int32).at[storage_slot_adapter].set(jnp.arange(ADAPTER_COUNT, dtype=jnp.int32))
    slot_index = storage[slot_request_adapter]

    def adapt(item_pack):
        token_row_block, selected_slot = item_pack
        down_factor_rows = jnp.dot(token_row_block, adapter_down_factors[selected_slot], preferred_element_type=jnp.float32).astype(jnp.bfloat16)
        return (jnp.dot(down_factor_rows[:, :ADAPTER_RANK], adapter_up_query[selected_slot], preferred_element_type=jnp.float32), jnp.dot(down_factor_rows[:, ADAPTER_RANK:], adapter_up_key_value[selected_slot], preferred_element_type=jnp.float32))
    delta_q, delta_kv = lax.map(adapt, (moved, slot_index))
    old_length = lengths[migration]
    positions = old_length[:, None] + jnp.arange(STEPS, dtype=jnp.int32)[None, :]
    query = rotate((base_q + delta_q).reshape(REQUESTS, STEPS, QUERY_HEADS, HEAD_SIZE), positions[:, :, None]).astype(jnp.bfloat16)
    kv_raw = (base_kv + delta_kv).reshape(REQUESTS, STEPS, KEY_VALUE_HEADS, 2, HEAD_SIZE)
    fresh_keys = rotate(kv_raw[:, :, :, 0], positions[:, :, None]).astype(jnp.bfloat16)
    fresh_values = kv_raw[:, :, :, 1].astype(jnp.bfloat16)
    tables = previous_block_table[migration] + (migration // RQ_DEV)[:, None] * POOL

    def attend(item_pack):
        query_rows, new_keys, new_values, length_at, table_row = item_pack
        query_rows = lax.optimization_barrier(query_rows)
        pages = paged_cache_pool[table_row].reshape(LCAP, KEY_VALUE_HEADS, 2, HEAD_SIZE)
        place = jnp.arange(LCAP, dtype=jnp.int32)
        pages = jnp.where((place < length_at)[:, None, None, None], pages, jnp.zeros_like(pages))
        for step_at in range(STEPS):
            landing = (place == length_at + step_at)[:, None, None, None]
            arrived = jnp.stack([new_keys[step_at], new_values[step_at]], axis=1)
            pages = jnp.where(landing, arrived[None], pages)
        key_rows = pages[:, :, 0].astype(jnp.float32)
        value_rows = pages[:, :, 1].astype(jnp.float32)
        grouped = query_rows.reshape(STEPS, KEY_VALUE_HEADS, QUERY_HEADS // KEY_VALUE_HEADS, HEAD_SIZE).astype(jnp.float32)
        scores = jnp.einsum('sjgd,pjd->sjgp', grouped, key_rows) / math.sqrt(HEAD_SIZE)
        visible = (place[None, :] <= (length_at + jnp.arange(STEPS, dtype=jnp.int32))[:, None])[:, None, None, :]
        scores = jnp.where(visible, scores, -1e+30)
        top_score = lax.optimization_barrier(jnp.max(scores, axis=-1, keepdims=True))
        weights = jnp.where(visible, jnp.exp(scores - top_score), 0.0)
        probability = (weights / lax.optimization_barrier(jnp.sum(weights, axis=-1, keepdims=True))).astype(jnp.bfloat16)
        probability = lax.optimization_barrier(probability)
        mixed_out = jnp.einsum('sjgp,pjd->sjgd', probability.astype(jnp.float32), value_rows)
        return (mixed_out.astype(jnp.bfloat16).reshape(STEPS, QUERY_HEADS * HEAD_SIZE), pages.reshape(LCAP, 2 * KEY_VALUE_HEADS * HEAD_SIZE))
    attention, dense = lax.map(attend, (query, fresh_keys, fresh_values, old_length, tables))
    new_group = jnp.arange(REQUESTS, dtype=jnp.int32) // RQ_DEV
    target = moved_block_table + new_group[:, None] * POOL
    new_pool = jnp.zeros(paged_cache_pool.shape, jnp.bfloat16).at[target.reshape(-1)].set(dense.reshape(REQUESTS * MAXB, PAGE, 2 * KEY_VALUE_HEADS * HEAD_SIZE))
    return (attention, new_pool)
```

```python
import functools
import math

import jax
import jax.numpy as jnp
from jax import lax
from jax.experimental import pallas as pl
from jax.experimental.pallas import tpu as pltpu
from jax.sharding import PartitionSpec as P

HEAD = 128
THETA = 500000.0
MIB = 1 << 20

F32 = jnp.float32
BF16 = jnp.bfloat16
I32 = jnp.int32


def iota(shape, axis):
    return lax.broadcasted_iota(I32, shape, axis)


def col_to_row(col):
    n = col.shape[0]
    return jnp.sum(jnp.where(iota((n, n), 0) == iota((n, n), 1), col, 0), axis=0, keepdims=True)


def row_to_col(row, n, stretch=1):
    w = row.shape[1]
    return jnp.sum(
        jnp.where(iota((n, w), 1) == iota((n, w), 0) // stretch, row, 0), axis=1, keepdims=True
    )


def below(mask):
    n = mask.shape[1]
    tri = (iota((n, n), 0) < iota((n, n), 1)).astype(BF16)
    return jnp.dot(mask.astype(BF16), tri, preferred_element_type=F32).astype(I32)


def plan_kernel(me_ref, mig_ref, sra_ref, ssa_ref, len_ref, tok_ref, send_ref, own_ref, cand_ref, meta_ref):
    r = me_ref[0]
    groups, per = mig_ref.shape
    half = per // 2
    mig = mig_ref[...]
    grp, loc = mig // per, mig % per
    drow = iota((groups, per), 0)
    out_mask = ((grp == r) & (drow != r)).astype(I32)
    mine = jnp.sum(jnp.where(drow == r, mig, 0), axis=0, keepdims=True)
    g_in, loc_in = mine // per, mine % per
    in_mask = (g_in == drow).astype(I32)
    ranks = below(jnp.concatenate([out_mask, in_mask], axis=0))
    out_rank, in_ranks = ranks[:groups], ranks[groups:]
    in_rank = jnp.sum(in_mask * in_ranks, axis=0, keepdims=True)
    stay = g_in == r

    parts = []
    for d in range(groups):
        hit = (out_mask[d : d + 1] == 1) & (out_rank[d : d + 1] == iota((groups, per), 0))
        parts.append(jnp.sum(jnp.where(hit, loc[d : d + 1] + 1, 0), axis=1, keepdims=True))
    src_col = jnp.concatenate(parts, axis=0) - 1
    src_row = col_to_row(src_col)

    count = jnp.sum(jnp.where(drow == r, 0, in_mask), axis=1, keepdims=True)
    lane_u = iota((groups, half), 1)
    count_u = jnp.sum(jnp.where(iota((groups, half), 0) == lane_u // groups, count, 0), axis=0, keepdims=True)
    free = (lane_u[:1] % groups >= count_u).astype(I32)
    free_rank = jnp.where(free == 1, below(free), -1)
    free_col = row_to_col(free_rank, half)
    extra = jnp.sum(
        jnp.where(free_col == in_rank - half, iota((half, per), 0), 0), axis=0, keepdims=True
    )
    place = jnp.where(
        stay, jnp.where(in_rank < half, in_rank, half + extra), half + groups * g_in + in_rank
    )
    sel = place == iota((per, per), 0)

    def placed(row):
        return jnp.sum(jnp.where(sel, row, 0), axis=1, keepdims=True)

    slot_row = col_to_row(placed(iota((1, per), 1)))
    loc_row = col_to_row(placed(jnp.where(stay, loc_in, -1)))

    drow_sra = iota(sra_ref.shape, 0)
    sra = sra_ref[...]
    wanted = jnp.sum(jnp.where(drow_sra == r, sra, 0), axis=0, keepdims=True)
    ssa_col = row_to_col(ssa_ref[...], half)
    store = jnp.sum(jnp.where(ssa_col == wanted, iota((half, per), 0), 0), axis=0, keepdims=True)
    cand = jnp.where(store // groups == r, store % groups, groups + store // groups)
    cand_row = col_to_row(placed(cand))
    rows = per * 4
    cand_ref[...] = jnp.broadcast_to(row_to_col(cand_row, rows, 4), (rows, HEAD)).astype(BF16)
    picks = jnp.zeros((groups, 1), I32)
    for i in range(groups):
        mine_id = jnp.sum(jnp.where(iota((1, half), 1) == r * groups + i, ssa_ref[...], 0))
        used = jnp.max((sra == mine_id).astype(I32), axis=1, keepdims=True)
        picks = jnp.maximum(picks, used * i)
    pick_row = jnp.sum(
        jnp.where(iota((groups, per), 0) == iota((groups, per), 1), picks, 0), axis=0, keepdims=True
    )

    len_col = jnp.broadcast_to(row_to_col(len_ref[...], rows, 4), (rows, HEAD))
    tok = jnp.concatenate([tok_ref[...], len_col.astype(F32).astype(BF16)], axis=1)

    def rows_of(row, n):
        base = row_to_col(row, n, 4)
        at = 4 * base + iota((n, 1), 0) % 4
        pick = (jnp.broadcast_to(at, (n, rows)) == iota((n, rows), 1)) & (base >= 0)
        return jnp.dot(
            jnp.where(pick, 1.0, 0.0).astype(BF16), tok, preferred_element_type=F32
        ).astype(BF16)

    send_ref[...] = rows_of(src_row, rows // 2)
    own_ref[...] = rows_of(loc_row, rows)
    src_wide = jnp.sum(
        jnp.where(iota((half, per), 0) == iota((half, per), 1), src_col, 0), axis=0, keepdims=True
    )
    zero = jnp.zeros((groups - 4, per), I32)
    meta_ref[...] = jnp.concatenate([slot_row, loc_row, src_wide, pick_row, zero], axis=0)


def vspec():
    return pl.BlockSpec(memory_space=pltpu.VMEM)


def sspec():
    return pl.BlockSpec(memory_space=pltpu.SMEM)


def params(mib):
    return pltpu.CompilerParams(vmem_limit_bytes=mib * MIB)


def sds(shape, dtype):
    return jax.ShapeDtypeStruct(shape, dtype)


def plan(me, mig, sra, ssa, lengths, tok):
    rows = tok.shape[0]
    return pl.pallas_call(
        plan_kernel,
        out_shape=(
            sds((rows // 2, 640), BF16),
            sds((rows, 640), BF16),
            sds((rows, HEAD), BF16),
            sds((8, HEAD), I32),
        ),
        in_specs=[sspec()] + [vspec()] * 5,
        out_specs=(vspec(),) * 4,
        compiler_params=params(24),
        name="plan",
    )(me, mig, sra, ssa, lengths, tok)


def pack_adapters_kernel(meta_ref, *refs):
    n = len(refs) // 2
    for src, dst in zip(refs[:n], refs[n:]):
        dst[...] = src[...]


def pack_adapters(meta, down, up_q, up_kv, up_kv_other):
    arrays = (down, up_q, up_kv, up_kv_other)

    def spec_in(a):
        return pl.BlockSpec((1,) + a.shape[1:], lambda d, meta: (meta[3, d], 0, 0))

    def spec_out(a):
        return pl.BlockSpec((1,) + a.shape[1:], lambda d, meta: (d, 0, 0))

    return pl.pallas_call(
        pack_adapters_kernel,
        grid_spec=pltpu.PrefetchScalarGridSpec(
            num_scalar_prefetch=1,
            grid=(8,),
            in_specs=[spec_in(a) for a in arrays],
            out_specs=tuple(spec_out(a) for a in arrays),
        ),
        out_shape=tuple(sds(a.shape, a.dtype) for a in arrays),
        name="pack_adapters",
    )(meta, *arrays)


def pack_cache_kernel(meta_ref, table_ref, pool_ref, out_ref):
    def one(u, _):
        src = jnp.maximum(meta_ref[2, u], 0)
        for b in range(8):
            out_ref[u * 8 + b] = pool_ref[table_ref[src, b]]
        return 0

    lax.fori_loop(0, 64, one, 0)


def pack_cache(meta, table, pool):
    return pl.pallas_call(
        pack_cache_kernel,
        out_shape=sds((512, 16, HEAD), BF16),
        in_specs=[sspec(), sspec(), vspec()],
        out_specs=vspec(),
        compiler_params=params(16),
        name="pack_cache",
    )(meta, table, pool)


def join_kernel(own_ref, got_ref, x_ref, len_ref, lens_ref):
    rows = x_ref.shape[0]
    x_ref[: rows // 2] = own_ref[: rows // 2, :512]
    x_ref[rows // 2 :] = own_ref[rows // 2 :, :512] + got_ref[:, :512]
    length = jnp.concatenate(
        [own_ref[: rows // 2, 512:], own_ref[rows // 2 :, 512:] + got_ref[:, 512:]], axis=0
    ).astype(F32)
    len_ref[...] = length
    row = jnp.sum(
        jnp.where(iota((rows, HEAD), 0) == 4 * iota((rows, HEAD), 1), length, 0.0),
        axis=0,
        keepdims=True,
    ).astype(I32)
    lens_ref[...] = jnp.broadcast_to(row, (8, HEAD))


def join(own, got):
    rows = own.shape[0]
    return pl.pallas_call(
        join_kernel,
        out_shape=(sds((rows, 512), BF16), sds((rows, HEAD), F32), sds((8, HEAD), I32)),
        in_specs=[vspec()] * 2,
        out_specs=(vspec(),) * 3,
        compiler_params=params(16),
        name="join",
    )(own, got)


def matmul_kernel(n, halves, js_ref, *refs):
    xs = refs[:n]
    i = n
    ws = [refs[i + 4 * k : i + 4 * k + 4] for k in range(len(halves))]
    i += 4 * len(halves)
    first = len(refs) - i == 2
    own_ref, far_ref = refs[-2:]
    own = far = None
    at = 0
    for k, parts in enumerate(halves):
        block = [x[...] for x in xs[at : at + parts]]
        at += parts
        x = block[0] if parts == 1 else jnp.concatenate(block, axis=0)
        wq, wk, vq, vk = ws[k]
        a = jnp.dot(x, wq[...], preferred_element_type=F32)
        b = jnp.concatenate(
            [
                jnp.dot(x, vq[...], preferred_element_type=F32),
                jnp.dot(
                    x, jnp.concatenate([wk[...], vk[...]], axis=1), preferred_element_type=F32
                ),
            ],
            axis=1,
        )
        own = a if own is None else own + a
        far = b if far is None else far + b
    if not first:
        own = own + refs[i][...]
        far = far + refs[i + 1][...]
    own_ref[...] = own
    far_ref[...] = far


def matmul(js, blocks, wq, wk, vq, vk, acc=None):
    nb = len(blocks)
    halves = [len(b) for b in blocks]
    xs = [x for b in blocks for x in b]
    specs = [pl.BlockSpec(x.shape, lambda s, js: (0, 0)) for x in xs]
    args = list(xs)
    for k in range(nb):
        for w, kind in ((wq, 0), (wk, 0), (vq, 1), (vk, 1)):
            specs.append(
                pl.BlockSpec((512, w.shape[1]), lambda s, js, k=k, kind=kind: (js[kind * nb + k], 0))
            )
            args.append(w)
    outs = [(512, 512), (512, 768)]
    if acc is not None:
        for a in acc:
            specs.append(pl.BlockSpec(a.shape, lambda s, js: (0, 0)))
            args.append(a)
    return pl.pallas_call(
        functools.partial(matmul_kernel, len(xs), halves),
        grid_spec=pltpu.PrefetchScalarGridSpec(
            num_scalar_prefetch=1,
            grid=(1,),
            in_specs=specs,
            out_specs=tuple(pl.BlockSpec(o, lambda s, js: (0, 0)) for o in outs),
        ),
        out_shape=tuple(sds(o, F32) for o in outs),
        compiler_params=params(48),
        name="matmul%d" % nb,
    )(js, *args)


def down_kernel(x_ref, here_ref, far_ref, cand_ref, out_ref):
    x = x_ref[...]
    cand = cand_ref[...].astype(F32)
    acc = None
    for a in range(16):
        ref = here_ref if a < 8 else far_ref
        y = jnp.dot(x, ref[a % 8], preferred_element_type=F32)
        y = jnp.where(cand == float(a), y, 0.0)
        acc = y if acc is None else acc + y
    out_ref[...] = acc


def down_product(x, here, far, cand):
    return pl.pallas_call(
        down_kernel,
        out_shape=sds((x.shape[0], HEAD), F32),
        in_specs=[vspec()] * 4,
        out_specs=vspec(),
        compiler_params=params(24),
        name="down_product",
    )(x, here, far, cand)


def down_sum_kernel(x_ref, out_ref):
    n = x_ref.shape[0]
    total = x_ref[0]
    for i in range(1, n):
        total = total + x_ref[i]
    total = total.astype(BF16)
    for i in range(n):
        out_ref[i] = total


def down_sum(x):
    return pl.pallas_call(
        down_sum_kernel,
        out_shape=sds(x.shape, BF16),
        in_specs=[vspec()],
        out_specs=vspec(),
        name="down_sum",
    )(x)


def up_kernel(down_ref, cand_ref, q_here, k_here, o_here, q_far, k_far, o_far, out_ref):
    down = down_ref[...].astype(F32)
    cand = cand_ref[...].astype(F32)
    rows = down.shape[0]
    lane = iota((rows, HEAD), 1)
    upper = lane >= HEAD // 2
    other = pltpu.roll(down, HEAD // 2, 1)
    down_q = jnp.where(upper, other, down)
    down_k = jnp.where(upper, down, other)
    shift = jnp.where(upper, 1.0, 0.0)

    def spread(v):
        return jnp.concatenate(
            [jnp.where(cand == shift + float(2 * i), v, 0.0).astype(BF16) for i in range(8)], axis=1
        )

    sq, sk = spread(down_q), spread(down_k)

    def both(here, far):
        h, f = here[...], far[...]
        return jnp.concatenate([h.reshape(-1, h.shape[2]), f.reshape(-1, f.shape[2])], axis=0)

    out_ref[:, :512] = jnp.dot(sq, both(q_here, q_far), preferred_element_type=F32)
    out_ref[:, 512:640] = jnp.dot(sk, both(k_here, k_far), preferred_element_type=F32)
    out_ref[:, 640:] = jnp.dot(sk, both(o_here, o_far), preferred_element_type=F32)


def up_product(down, cand, here, far):
    return pl.pallas_call(
        up_kernel,
        out_shape=sds((down.shape[0], 768), F32),
        in_specs=[vspec()] * 8,
        out_specs=vspec(),
        compiler_params=params(24),
        name="up_product",
    )(down, cand, *here, *far)


def attend_kernel(
    par_ref, meta_ref, lens_ref, prev_ref, moved_ref,
    own_ref, far_ref, rx_ref, delta_ref, cos_ref, sin_ref,
    pool_ref, pool2_ref, got_ref, got2_ref,
    out_ref, new_ref,
    q_scr, f_scr, kv_scr,
):
    odd = par_ref[0]
    cos, sin = cos_ref[...], sin_ref[...]

    def turn(v):
        return v * cos + pltpu.roll(v, HEAD // 2, 1) * sin

    for h in range(4):
        at = slice(h * HEAD, (h + 1) * HEAD)
        q_scr[:, at] = turn(own_ref[:, at] + rx_ref[:, at] + delta_ref[:, at])
    kv_own = far_ref[:, 512:640] + rx_ref[:, 640:768] + delta_ref[:, 512:640]
    kv_oth = far_ref[:, 640:768] + rx_ref[:, 512:640] + delta_ref[:, 640:768]
    key = turn(jnp.where(odd == 0, kv_own, kv_oth))
    value = jnp.where(odd == 0, kv_oth, kv_own)
    f_scr[:, :HEAD] = key
    f_scr[:, HEAD:] = value

    t = iota((256, 8), 0)
    c = iota((256, 8), 1)
    t_wide = iota((HEAD, HEAD), 0)
    row2 = (iota((32, 256), 0) % 8) // 4
    step = iota((32, 256), 0) % 4
    col = iota((32, 256), 1)

    def pair(i, arrivals):
        lengths, slots = [], []
        for e in range(2):
            p = 2 * i + e
            n = meta_ref[0, p]
            lengths.append(lens_ref[0, p])
            slots.append(n)
            src = meta_ref[1, p]
            local = jnp.maximum(src, 0)
            for b in range(8):
                page = prev_ref[local, b]
                mine, other = pool_ref[page], pool2_ref[page]
                if arrivals:
                    at = (p - 64) * 8 + b
                    mine = jnp.where(src < 0, got_ref[at], mine)
                    other = jnp.where(src < 0, got2_ref[at], other)
                rows = pl.ds(e * HEAD + b * 16, 16)
                kv_scr[0, rows, :] = mine
                kv_scr[1, rows, :] = other
        fresh = f_scr[pl.ds(pl.multiple_of(8 * i, 8), 8), :].astype(BF16)
        land = (t % HEAD == jnp.where(c < 4, lengths[0], lengths[1]) + c % 4) & (t // HEAD == c // 4)
        spread = jnp.dot(
            jnp.where(land, 1.0, 0.0).astype(BF16), fresh, preferred_element_type=F32
        )
        old = jnp.concatenate(
            [t_wide < lengths[0], t_wide < lengths[1]], axis=0
        )
        keys = jnp.where(old, kv_scr[odd].astype(F32), spread[:, :HEAD]).astype(BF16)
        values = jnp.where(old, kv_scr[1 - odd].astype(F32), spread[:, HEAD:]).astype(BF16)
        kept = jnp.where(odd == 0, keys, values)
        for e in range(2):
            for b in range(8):
                lo = e * HEAD + b * 16
                new_ref[moved_ref[slots[e], b]] = kept[lo : lo + 16]
        q = q_scr[pl.ds(pl.multiple_of(8 * i, 8), 8), :]
        q = jnp.concatenate([q[:, h * HEAD : (h + 1) * HEAD] for h in range(4)], axis=0)
        scores = lax.dot_general(
            q.astype(BF16), keys, (((1,), (1,)), ((), ())), preferred_element_type=F32
        ) / math.sqrt(HEAD)
        limit = jnp.where(row2 == 0, lengths[0], lengths[1] + HEAD) + step
        seen = (col <= limit) & (col >= row2 * HEAD)
        scores = jnp.where(seen, scores, -1e30)
        top = jnp.max(scores, axis=1, keepdims=True)
        weight = jnp.where(seen, jnp.exp(scores - top), 0.0)
        prob = (weight / jnp.sum(weight, axis=1, keepdims=True)).astype(BF16)
        mixed = jnp.dot(prob, values, preferred_element_type=F32)
        for e in range(2):
            for h in range(4):
                lo = h * 8 + e * 4
                out_ref[slots[e], :, h * HEAD : (h + 1) * HEAD] = mixed[lo : lo + 4].astype(BF16)

    def first(i, _):
        pair(i, False)
        return 0

    def second(i, _):
        pair(i, True)
        return 0

    lax.fori_loop(0, 32, first, 0)
    lax.fori_loop(32, 64, second, 0)


def attend(parity, meta, lens, prev, moved, own, far, rx, delta, cos, sin, pool, pool2, got, got2):
    return pl.pallas_call(
        attend_kernel,
        out_shape=(sds((128, 4, 512), BF16), sds((1024, 16, HEAD), BF16)),
        in_specs=[sspec()] * 5 + [vspec()] * 10,
        out_specs=(vspec(), vspec()),
        scratch_shapes=[
            pltpu.VMEM((512, 512), F32),
            pltpu.VMEM((512, 256), F32),
            pltpu.VMEM((2, 256, HEAD), BF16),
        ],
        compiler_params=params(40),
        name="attend",
    )(parity, meta, lens, prev, moved, own, far, rx, delta, cos, sin, pool, pool2, got, got2)


def body(
    tokens,
    query_weight_matrix,
    key_value_weight,
    adapter_down_factors,
    adapter_up_query,
    adapter_up_key_value,
    storage_slot_adapter,
    slot_request_adapter,
    migration,
    lengths,
    previous_block_table,
    moved_block_table,
    paged_cache_pool,
):
    r = lax.axis_index("rep").astype(I32)
    t = lax.axis_index("tp").astype(I32)
    core = t % 2

    def other_core(a):
        return lax.ppermute(a, "tp", [(i, i ^ 1) for i in range(16)])

    def other_x(a):
        return lax.ppermute(a, "tp", [(i, i ^ 2) for i in range(16)])

    def along_y(a, d):
        return lax.ppermute(a, "tp", [(i, (i + 4 * d) % 16) for i in range(16)])

    def swap_rep(a):
        return lax.all_to_all(a, "rep", split_axis=0, concat_axis=0, tiled=True)

    send, own, cand, meta = plan(
        r.reshape(1),
        migration.reshape(8, 128),
        slot_request_adapter.reshape(8, 128),
        storage_slot_adapter.reshape(1, 64),
        lengths.reshape(1, 128),
        tokens.reshape(512, 512),
    )
    x, length, lens = join(own, swap_rep(send))

    pool2 = other_core(paged_cache_pool)
    far_core = 1 - core
    vq = other_core(
        lax.dynamic_index_in_dim(query_weight_matrix.reshape(8, 2, 512, 512), far_core, 1, False)
    ).reshape(4096, 512)
    vk = other_core(
        lax.dynamic_index_in_dim(key_value_weight.reshape(8, 2, 512, HEAD), far_core, 1, False)
    ).reshape(4096, HEAD)
    up_kv_other = other_core(adapter_up_key_value)

    here = (adapter_up_query, adapter_up_key_value, up_kv_other)
    packed = pack_adapters(meta, adapter_down_factors, *here)
    far_down = swap_rep(packed[0])
    far_up = tuple(swap_rep(a) for a in packed[1:])
    got = swap_rep(pack_cache(meta, previous_block_table, paged_cache_pool))
    got2 = other_core(got)

    hi = (t // 2) % 2
    y = t // 4

    def rows(dy, dx):
        at = ((y + dy) % 4) * 2 + (hi ^ dx)
        return at * 2 + core, at

    def js(*blocks):
        pairs = [rows(*b) for b in blocks]
        return jnp.stack([p[0] for p in pairs] + [p[1] for p in pairs]).astype(I32)

    weights = (query_weight_matrix, key_value_weight, vq, vk)
    xh = other_x(x)
    yp = along_y(x, 1)
    ym = along_y(x, -1)
    xyp = along_y(xh, 1)
    xym = along_y(xh, -1)
    y2 = (along_y(yp[:256], 1), along_y(ym[256:], -1))
    acc = matmul(js((0, 0), (0, 1), (3, 0), (1, 0)), [(x,), (xh,), (yp,), (ym,)], *weights)
    xy2 = (along_y(xyp[:256], 1), along_y(xym[256:], -1))
    acc = matmul(js((3, 1), (1, 1), (2, 0)), [(xyp,), (xym,), y2], *weights, acc=acc)
    acc_own, acc_far = matmul(js((2, 1)), [xy2], *weights, acc=acc)
    rx = other_core(acc_far)

    partial = down_product(x, adapter_down_factors, far_down, cand)
    pieces = lax.all_to_all(partial, "tp", split_axis=0, concat_axis=0, tiled=True)
    down = lax.all_to_all(
        down_sum(pieces.reshape(16, 32, HEAD)).reshape(512, HEAD),
        "tp", split_axis=0, concat_axis=0, tiled=True,
    )
    delta = up_product(down, cand, here, far_up)

    positions = length + (jnp.arange(512, dtype=I32) % 4).astype(F32)[:, None]
    frequency = THETA ** (-(jnp.arange(HEAD // 2, dtype=F32) * 2.0 / HEAD))
    angles = positions[:, : HEAD // 2] * frequency
    cos, sin = jnp.cos(angles), jnp.sin(angles)
    cos = jnp.concatenate([cos, cos], axis=1)
    sin = jnp.concatenate([-sin, sin], axis=1)
    return attend(
        core.reshape(1), meta, lens, previous_block_table, moved_block_table,
        acc_own, acc_far, rx, delta, cos, sin, paged_cache_pool, pool2, got, got2,
    )


def solution(mesh):
    in_specs = (
        P("rep", None, "tp"),
        P(None, "tp"),
        P(None, "tp"),
        P("rep", "tp", None),
        P("rep", None, "tp"),
        P("rep", None, "tp"),
        P(),
        P(),
        P(),
        P("rep"),
        P("rep", None),
        P("rep", None),
        P("rep", None, "tp"),
    )
    out_specs = (P("rep", None, "tp"), P("rep", None, "tp"))
    return jax.shard_map(body, mesh=mesh, in_specs=in_specs, out_specs=out_specs, check_vma=False)
```

```python
import functools
import math

import jax
import jax.numpy as jnp
import ml_dtypes
import numpy as np
from jax import lax
from jax.experimental import pallas as pl
from jax.experimental.pallas import tpu as pltpu
from jax.sharding import PartitionSpec as P

HEAD = 128
THETA = 500000.0
MIB = 1 << 20
VMEM_MIB = 60
POOL = 1024
ZERO_PAGE = POOL + 512

SLOT, PICK, SOURCE, TARGET, LEAVE = 0, 3, 8, 16, 24
KEPT, LENGTH, FROM = 0, 8, 16

F32 = jnp.float32
BF16 = jnp.bfloat16
I32 = jnp.int32


def iota(shape, axis):
    return lax.broadcasted_iota(I32, shape, axis)


def col_to_row(col):
    n = col.shape[0]
    return jnp.sum(jnp.where(iota((n, n), 0) == iota((n, n), 1), col, 0), axis=0, keepdims=True)


def row_to_col(row, n, stretch=1):
    w = row.shape[1]
    return jnp.sum(
        jnp.where(iota((n, w), 1) == iota((n, w), 0) // stretch, row, 0), axis=1, keepdims=True
    )


def below(mask):
    n = mask.shape[1]
    tri = (iota((n, n), 0) < iota((n, n), 1)).astype(BF16)
    return jnp.dot(mask.astype(BF16), tri, preferred_element_type=F32).astype(I32)


def plan_kernel(
    me_ref, mig_hbm, sra_hbm, ssa_hbm, len_hbm, prev_hbm, moved_hbm, tok_hbm,
    send_hbm, own_hbm, cand_hbm, meta_hbm,
    mig_ref, sra_ref, ssa_ref, len_ref, prev_ref, moved_ref, tok_ref, send_ref, own_ref, cand_ref, meta_ref, sem,
):
    loads = fetch(
        (
            (mig_hbm, mig_ref), (sra_hbm, sra_ref), (ssa_hbm, ssa_ref), (len_hbm, len_ref),
            (prev_hbm, prev_ref), (moved_hbm, moved_ref), (tok_hbm, tok_ref),
        ),
        sem,
    )
    settle(loads[:6])
    r = me_ref[0]
    groups, per = mig_ref.shape
    half = per // 2
    mig = mig_ref[...]
    grp, loc = mig // per, mig % per
    drow = iota((groups, per), 0)
    out_mask = ((grp == r) & (drow != r)).astype(I32)
    mine = jnp.sum(jnp.where(drow == r, mig, 0), axis=0, keepdims=True)
    g_in, loc_in = mine // per, mine % per
    in_mask = (g_in == drow).astype(I32)
    ranks = below(jnp.concatenate([out_mask, in_mask], axis=0))
    out_rank, in_ranks = ranks[:groups], ranks[groups:]
    in_rank = jnp.sum(in_mask * in_ranks, axis=0, keepdims=True)
    stay = g_in == r

    parts = []
    for d in range(groups):
        hit = (out_mask[d : d + 1] == 1) & (out_rank[d : d + 1] == iota((groups, per), 0))
        parts.append(jnp.sum(jnp.where(hit, loc[d : d + 1] + 1, 0), axis=1, keepdims=True))
    src_col = jnp.concatenate(parts, axis=0) - 1
    src_row = col_to_row(src_col)

    count = jnp.sum(jnp.where(drow == r, 0, in_mask), axis=1, keepdims=True)
    lane_u = iota((groups, half), 1)
    count_u = jnp.sum(jnp.where(iota((groups, half), 0) == lane_u // groups, count, 0), axis=0, keepdims=True)
    free = (lane_u[:1] % groups >= count_u).astype(I32)
    free_rank = jnp.where(free == 1, below(free), -1)
    free_col = row_to_col(free_rank, half)
    extra = jnp.sum(
        jnp.where(free_col == in_rank - half, iota((half, per), 0), 0), axis=0, keepdims=True
    )
    place = jnp.where(
        stay, jnp.where(in_rank < half, in_rank, half + extra), half + groups * g_in + in_rank
    )
    sel = place == iota((per, per), 0)

    def placed(row):
        return jnp.sum(jnp.where(sel, row, 0), axis=1, keepdims=True)

    slot_row = col_to_row(placed(iota((1, per), 1)))
    loc_row = col_to_row(placed(jnp.where(stay, loc_in, -1)))

    drow_sra = iota(sra_ref.shape, 0)
    sra = sra_ref[...]
    wanted = jnp.sum(jnp.where(drow_sra == r, sra, 0), axis=0, keepdims=True)
    ssa_col = row_to_col(ssa_ref[...], half)
    store = jnp.sum(jnp.where(ssa_col == wanted, iota((half, per), 0), 0), axis=0, keepdims=True)
    cand = jnp.where(store // groups == r, store % groups, groups + store // groups)
    cand_row = col_to_row(placed(cand))
    rows = per * 4
    cand_ref[...] = jnp.broadcast_to(row_to_col(cand_row, rows, 4), (rows, HEAD)).astype(BF16)
    picks = jnp.zeros((groups, 1), I32)
    lane_s = iota((1, half), 1)
    for i in range(groups):
        name = jnp.sum(jnp.where(lane_s == r * groups + i, ssa_ref[...], 0), axis=1, keepdims=True)
        used = jnp.max((sra == name).astype(I32), axis=1, keepdims=True)
        picks = jnp.maximum(picks, used * i)
    pick_row = jnp.sum(
        jnp.where(iota((groups, per), 0) == iota((groups, per), 1), picks, 0), axis=0, keepdims=True
    )

    len_col = jnp.broadcast_to(row_to_col(len_ref[...], rows, 4), (rows, HEAD))
    settle(loads[6:])
    tok = jnp.concatenate([tok_ref[...], len_col.astype(F32).astype(BF16)], axis=1)

    def rows_of(row, n):
        base = row_to_col(row, n, 4)
        at = 4 * base + iota((n, 1), 0) % 4
        pick = (jnp.broadcast_to(at, (n, rows)) == iota((n, rows), 1)) & (base >= 0)
        return jnp.dot(
            jnp.where(pick, 1.0, 0.0).astype(BF16), tok, preferred_element_type=F32
        ).astype(BF16)

    send_ref[...] = rows_of(src_row, rows // 2)
    stores = fetch(((send_ref, send_hbm),), sem)
    own_ref[...] = rows_of(loc_row, rows)
    stores += fetch(((own_ref, own_hbm),), sem, 1)
    src_wide = jnp.sum(
        jnp.where(iota((half, per), 0) == iota((half, per), 1), src_col, 0), axis=0, keepdims=True
    )
    def looked_up(table, row):
        pick = jnp.where(row == iota((per, per), 0), 1.0, 0.0).astype(BF16)
        parts = jnp.concatenate([table // 32, table % 32], axis=0).astype(F32).astype(BF16)
        found = jnp.dot(parts, pick, preferred_element_type=F32).astype(I32)
        return found[:8] * 32 + found[8:]

    prev, moved = prev_ref[...], moved_ref[...]
    lane8, row8 = iota((8, per), 1), iota((8, per), 0)
    source = jnp.where(loc_row >= 0, looked_up(prev, loc_row), POOL + (lane8 - half) * 8 + row8)
    target = looked_up(moved, slot_row)
    leave = looked_up(prev, src_wide)
    zero = jnp.zeros((groups - 4, per), I32)
    meta_ref[...] = jnp.concatenate(
        [slot_row, loc_row, src_wide, pick_row, zero, source, target, leave], axis=0
    )
    stores += fetch(((cand_ref, cand_hbm), (meta_ref, meta_hbm)), sem, 2)
    settle(stores)


def hspec():
    return pl.BlockSpec(memory_space=pltpu.HBM)


def fetch(pairs, sem, at=0):
    copies = [pltpu.make_async_copy(a, b, sem.at[at + n]) for n, (a, b) in enumerate(pairs)]
    for c in copies:
        c.start()
    return copies


def settle(copies):
    for c in copies:
        c.wait()


def sspec():
    return pl.BlockSpec(memory_space=pltpu.SMEM)


def params():
    return pltpu.CompilerParams(vmem_limit_bytes=VMEM_MIB * MIB)


def sds(shape, dtype):
    return jax.ShapeDtypeStruct(shape, dtype)


def plan(me, mig, sra, ssa, lengths, prev, moved, tok):
    rows = tok.shape[0]
    ins = (mig, sra, ssa, lengths, prev, moved, tok)
    outs = (
        sds((rows // 2, 640), BF16),
        sds((rows, 640), BF16),
        sds((rows, HEAD), BF16),
        sds((32, HEAD), I32),
    )
    return pl.pallas_call(
        plan_kernel,
        out_shape=outs,
        in_specs=[sspec()] + [hspec()] * 7,
        out_specs=(hspec(),) * 4,
        scratch_shapes=[pltpu.VMEM(a.shape, a.dtype) for a in ins + outs]
        + [pltpu.SemaphoreType.DMA((7,))],
        compiler_params=params(),
        name="plan",
    )(me, *ins)


def pack_adapters_kernel(meta_ref, down_hbm, q_hbm, k_hbm, out_hbm, q_ref, out_ref, sem):
    pairs = []
    for d in range(8):
        i = meta_ref[PICK, d]
        pairs.append((q_hbm.at[i], q_ref.at[d]))
        pairs.append((k_hbm.at[i], out_ref.at[d, 768:]))
        pairs.append((down_hbm.at[i], out_ref.at[d, :512]))
    loads = fetch(pairs, sem)
    for d in range(8):
        loads[3 * d].wait()
        q = q_ref[d]
        for h in range(4):
            out_ref[d, 512 + 64 * h : 576 + 64 * h] = q[:, h * HEAD : (h + 1) * HEAD]
        loads[3 * d + 1].wait()
        loads[3 * d + 2].wait()
    settle(fetch(((out_ref, out_hbm),), sem))


def pack_adapters(meta, down, up_q, up_kv):
    return pl.pallas_call(
        pack_adapters_kernel,
        out_shape=sds((8, 832, HEAD), BF16),
        in_specs=[sspec()] + [hspec()] * 3,
        out_specs=hspec(),
        scratch_shapes=[
            pltpu.VMEM(up_q.shape, BF16),
            pltpu.VMEM((8, 832, HEAD), BF16),
            pltpu.SemaphoreType.DMA((24,)),
        ],
        compiler_params=params(),
        name="pack_adapters",
    )(meta, down, up_q, up_kv)


def pack_cache_kernel(meta_ref, pool_hbm, cache_hbm, pool_ref, cache_ref, sem):
    settle(fetch(((pool_hbm, pool_ref),), sem))

    def some(g, _):
        pages = [pool_ref[meta_ref[LEAVE + b, 4 * g + e]] for e in range(4) for b in range(8)]
        for n, page in enumerate(pages):
            cache_ref[g * 32 + n] = page
        return 0

    lax.fori_loop(0, 16, some, 0)
    settle(fetch(((cache_ref, cache_hbm),), sem))


def pack_cache(meta, pool):
    return pl.pallas_call(
        pack_cache_kernel,
        out_shape=sds((512, 16, HEAD), BF16),
        in_specs=[sspec(), hspec()],
        out_specs=hspec(),
        scratch_shapes=[
            pltpu.VMEM(pool.shape, BF16),
            pltpu.VMEM((512, 16, HEAD), BF16),
            pltpu.SemaphoreType.DMA((1,)),
        ],
        compiler_params=params(),
        name="pack_cache",
    )(meta, pool)


def join_kernel(
    own_hbm, got_hbm, meta_hbm, after_ref, after2_ref, after3_ref, x_hbm, len_hbm, lens_hbm,
    own_ref, got_ref, meta_ref, x_ref, len_ref, lens_ref, sem,
):
    settle(fetch(((own_hbm, own_ref), (got_hbm, got_ref), (meta_hbm, meta_ref)), sem))
    rows = x_ref.shape[0]
    x_ref[: rows // 2] = own_ref[: rows // 2, :512]
    x_ref[rows // 2 :] = own_ref[rows // 2 :, :512] + got_ref[:, :512]
    store = fetch(((x_ref, x_hbm),), sem)
    length = jnp.concatenate(
        [own_ref[: rows // 2, 512:], own_ref[rows // 2 :, 512:] + got_ref[:, 512:]], axis=0
    ).astype(F32)
    len_ref[...] = length
    row = jnp.sum(
        jnp.where(iota((rows, HEAD), 0) == 4 * iota((rows, HEAD), 1), length, 0.0),
        axis=0,
        keepdims=True,
    ).astype(I32)
    kept = jnp.clip(row - 16 * iota((8, HEAD), 0), 0, 16)
    lens_ref[KEPT : KEPT + 8] = kept
    lens_ref[LENGTH : LENGTH + 8] = jnp.broadcast_to(row, (8, HEAD))
    lens_ref[FROM : FROM + 8] = jnp.where(kept > 0, meta_ref[SOURCE : SOURCE + 8], ZERO_PAGE)
    settle(store + fetch(((len_ref, len_hbm), (lens_ref, lens_hbm)), sem, 1))


def join(own, got, meta, *after):
    rows = own.shape[0]
    return pl.pallas_call(
        join_kernel,
        out_shape=(sds((rows, 512), BF16), sds((rows, HEAD), F32), sds((24, HEAD), I32)),
        in_specs=[hspec()] * 6,
        out_specs=(hspec(),) * 3,
        scratch_shapes=[
            pltpu.VMEM(own.shape, BF16),
            pltpu.VMEM(got.shape, BF16),
            pltpu.VMEM(meta.shape, I32),
            pltpu.VMEM((rows, 512), BF16),
            pltpu.VMEM((rows, HEAD), F32),
            pltpu.VMEM((24, HEAD), I32),
            pltpu.SemaphoreType.DMA((3,)),
        ],
        compiler_params=params(),
        name="join",
    )(own, got, meta, *after)


def slices_kernel(moves, n, *refs):
    outs = len({m[2] for m in moves})
    ins, dst = refs[:n], refs[-1 - 2 * outs : -1 - outs]
    tmp, sem = refs[-1 - outs : -1], refs[-1]
    loads = fetch(
        [(ins[i].at[lo:hi], tmp[o].at[at : at + hi - lo]) for i, (lo, hi), o, at in moves], sem
    )
    settle(loads)
    settle(fetch([(t, d) for t, d in zip(tmp, dst)], sem))


def slices(moves, rows, arrays, after):
    shapes = [(n, 512) for n in rows]
    return pl.pallas_call(
        functools.partial(slices_kernel, moves, len(arrays)),
        out_shape=tuple(sds(s, BF16) for s in shapes),
        in_specs=[hspec()] * (len(arrays) + len(after)),
        out_specs=(hspec(),) * len(rows),
        scratch_shapes=[pltpu.VMEM(s, BF16) for s in shapes]
        + [pltpu.SemaphoreType.DMA((len(moves),))],
        compiler_params=params(),
        name="slices",
    )(*arrays, *after)


def matmul_kernel(blocks, n, extra, js_ref, *refs):
    xs, refs = refs[:n], refs[n:]
    weights, refs = refs[:4], refs[4:]
    accs, refs = refs[:extra], refs[extra:]
    own_hbm, far_hbm, refs = refs[0], refs[1], refs[2:]
    bufs, refs = refs[:4], refs[4:]
    held, refs = refs[:n], refs[n:]
    acc, refs = refs[:extra], refs[extra:]
    own_ref, far_ref, x_sem, sem, acc_sem = refs
    nb = len(blocks)
    loads = fetch(list(zip(xs, held)), x_sem)
    copies = []
    for k in range(nb):
        at = pl.ds(pl.multiple_of(js_ref[k] * 512, 512), 512)
        copies.append(
            [
                pltpu.make_async_copy(
                    weights[w].at[at], bufs[w].at[k * 512 : (k + 1) * 512], sem.at[k, w]
                )
                for w in range(4)
            ]
        )
    for w in (2, 1, 3, 0):
        for k in range(nb):
            copies[k][w].start()
    acc_loads = fetch(list(zip(accs, acc)), acc_sem)
    settle(loads)
    x = []
    for parts in blocks:
        pieces = [held[i][lo:hi] for i, lo, hi in parts]
        x.append(pieces[0] if len(pieces) == 1 else jnp.concatenate(pieces, axis=0))
    x = jnp.concatenate(x, axis=1) if nb > 1 else x[0]

    def product(*which):
        for k in range(nb):
            for w in which:
                copies[k][w].wait()
        w = [bufs[w][...] for w in which]
        w = w[0] if len(w) == 1 else jnp.concatenate(w, axis=1)
        return jnp.dot(x, w, preferred_element_type=F32)

    far_q = product(2)
    settle(acc_loads)
    if extra:
        far_q = far_q + acc[1][:, :512]
    far_ref[:, :512] = far_q
    far_k = product(1, 3)
    if extra:
        far_k = far_k + acc[1][:, 512:]
    if extra == 3:
        far_k = far_k + jnp.concatenate([acc[2][:, 512:], jnp.zeros((512, HEAD), F32)], axis=1)
    far_ref[:, 512:] = far_k
    stores = fetch(((far_ref, far_hbm),), acc_sem, extra)
    own = product(0)
    if extra:
        own = own + acc[0][...]
    if extra == 3:
        own = own + acc[2][:, :512]
    own_ref[...] = own
    settle(stores + fetch(((own_ref, own_hbm),), acc_sem, extra + 1))


def matmul(js, blocks, xs, weights, accs=()):
    nb = len(blocks)
    outs = (sds((512, 512), F32), sds((512, 768), F32))
    return pl.pallas_call(
        functools.partial(matmul_kernel, blocks, len(xs), len(accs)),
        out_shape=outs,
        in_specs=[sspec()] + [hspec()] * (len(xs) + 4 + len(accs)),
        out_specs=(hspec(), hspec()),
        scratch_shapes=[pltpu.VMEM((nb * 512, w.shape[1]), BF16) for w in weights]
        + [pltpu.VMEM(a.shape, a.dtype) for a in (*xs, *accs, *outs)]
        + [
            pltpu.SemaphoreType.DMA((len(xs),)),
            pltpu.SemaphoreType.DMA((nb, 4)),
            pltpu.SemaphoreType.DMA((len(accs) + 2,)),
        ],
        compiler_params=params(),
        name="matmul%d" % nb,
    )(js, *xs, *weights, *accs)


def down_kernel(
    core_ref, x_hbm, here_hbm, far_hbm, cand_hbm, keep_hbm, give_hbm,
    x_ref, here_ref, far_ref, cand_ref, out_ref, sem,
):
    loads = fetch(
        ((x_hbm, x_ref), (here_hbm, here_ref), (cand_hbm, cand_ref), (far_hbm.at[:, :512], far_ref)),
        sem,
    )
    settle(loads[:3])
    x = x_ref[...]
    cand = cand_ref[...].astype(F32)
    acc = None
    for a in range(0, 16, 2):
        if a == 8:
            settle(loads[3:])
        ref = here_ref if a < 8 else far_ref
        b = a % 8
        w = jnp.concatenate([ref[b], ref[b + 1]], axis=1)
        y = jnp.dot(x, w, preferred_element_type=F32)
        y = jnp.where(cand == float(a), y[:, :HEAD], jnp.where(cand == float(a + 1), y[:, HEAD:], 0.0))
        acc = y if acc is None else acc + y
    out_ref[...] = acc
    half = out_ref.shape[0] // 2
    mine = pl.ds(pl.multiple_of(core_ref[0] * half, half), half)
    other = pl.ds(pl.multiple_of((1 - core_ref[0]) * half, half), half)
    settle(fetch(((out_ref.at[mine], keep_hbm), (out_ref.at[other], give_hbm)), sem))


def down_product(core, x, here, far, cand):
    rows = x.shape[0]
    return pl.pallas_call(
        down_kernel,
        out_shape=(sds((rows // 2, HEAD), F32),) * 2,
        in_specs=[sspec()] + [hspec()] * 4,
        out_specs=(hspec(), hspec()),
        scratch_shapes=[
            pltpu.VMEM(x.shape, BF16),
            pltpu.VMEM(here.shape, BF16),
            pltpu.VMEM(here.shape, BF16),
            pltpu.VMEM(cand.shape, BF16),
            pltpu.VMEM((rows, HEAD), F32),
            pltpu.SemaphoreType.DMA((4,)),
        ],
        compiler_params=params(),
        name="down_product",
    )(core, x, here, far, cand)


def turn_table():
    frequency = np.float32(THETA) ** (-(np.arange(HEAD // 2, dtype=np.float32) * 2.0 / HEAD))
    angles = np.arange(HEAD, dtype=np.float32)[:, None] * frequency.astype(np.float32)
    cos, sin = np.cos(angles.astype(np.float64)), np.sin(angles.astype(np.float64))
    rest = np.concatenate([cos, cos, -sin, sin], axis=1).astype(np.float32)
    terms = []
    for _ in range(3):
        terms.append(rest.astype(ml_dtypes.bfloat16))
        rest = rest - terms[-1].astype(np.float32)
    return np.concatenate(terms, axis=1)


def up_kernel(
    core_ref, mine_hbm, other_hbm, far_hbm, cand_hbm, q_hbm, k_hbm, len_hbm, table_hbm, after_ref,
    out_hbm, cos_hbm, sin_hbm,
    down_ref, far, cand_ref, q_here, k_here, len_ref, table_ref, out_ref, cos_ref, sin_ref, sem,
):
    half = mine_hbm.shape[0]
    mine = pl.ds(pl.multiple_of(core_ref[0] * half, half), half)
    other = pl.ds(pl.multiple_of((1 - core_ref[0]) * half, half), half)
    settle(
        fetch(
            (
                (mine_hbm, down_ref.at[mine]), (other_hbm, down_ref.at[other]),
                (far_hbm.at[:, 512:], far), (cand_hbm, cand_ref), (q_hbm, q_here),
                (k_hbm, k_here), (len_hbm, len_ref), (table_hbm, table_ref),
            ),
            sem,
        )
    )
    down = down_ref[...].astype(F32)
    cand = cand_ref[...].astype(F32)
    rows = down.shape[0]
    lane = iota((rows, HEAD), 1)
    upper = lane >= HEAD // 2
    other = pltpu.roll(down, HEAD // 2, 1)
    down_q = jnp.where(upper, other, down)
    down_k = jnp.where(upper, down, other)
    shift = jnp.where(upper, 1.0, 0.0)

    def spread(v):
        return jnp.concatenate(
            [jnp.where(cand == shift + float(2 * i), v, 0.0).astype(BF16) for i in range(8)], axis=1
        )

    sq, sk = spread(down_q), spread(down_k)
    q_all, k_all = q_here[...].reshape(512, 512), k_here[...].reshape(512, HEAD)

    def far_part(lo):
        return jnp.concatenate([far[a, lo : lo + 64] for a in range(8)], axis=0)

    w = [
        jnp.concatenate([q_all[:, h * HEAD : (h + 1) * HEAD], far_part(64 * h)], axis=0)
        for h in range(4)
    ]
    for h in (0, 2):
        out_ref[:, h * HEAD : (h + 2) * HEAD] = jnp.dot(
            sq, jnp.concatenate([w[h], w[h + 1]], axis=1), preferred_element_type=F32
        )
    out_ref[:, 512:] = jnp.dot(
        sk, jnp.concatenate([k_all, far_part(256)], axis=0), preferred_element_type=F32
    )
    position = len_ref[...].astype(I32) + iota((rows, HEAD), 0) % 4
    pick = jnp.where(position == lane, 1.0, 0.0).astype(BF16)
    turns = jnp.dot(pick, table_ref[...], preferred_element_type=F32)
    turns = turns[:, :256] + turns[:, 256:512] + turns[:, 512:]
    cos_ref[...] = turns[:, :HEAD]
    sin_ref[...] = turns[:, HEAD:]
    settle(fetch(((out_ref, out_hbm), (cos_ref, cos_hbm), (sin_ref, sin_hbm)), sem))


def up_product(core, mine, other, far, cand, up_q, up_kv, length, after):
    rows = cand.shape[0]
    ins = (cand, up_q, up_kv, length, jnp.asarray(turn_table()))
    outs = (sds((rows, 640), F32), sds((rows, HEAD), F32), sds((rows, HEAD), F32))
    return pl.pallas_call(
        up_kernel,
        out_shape=outs,
        in_specs=[sspec()] + [hspec()] * 9,
        out_specs=(hspec(),) * 3,
        scratch_shapes=[pltpu.VMEM((rows, HEAD), BF16), pltpu.VMEM((8, 320, HEAD), BF16)]
        + [pltpu.VMEM(a.shape, a.dtype) for a in ins + outs]
        + [pltpu.SemaphoreType.DMA((8,))],
        compiler_params=params(),
        name="up_product",
    )(core, mine, other, far, *ins, after)


GROUP = 4


def page_masks(mask_scr):
    for d in range(17):
        mask_scr[d] = jnp.where(iota((16, HEAD), 0) < d, 1.0, 0.0).astype(BF16)


def attend_kernel(
    par_ref, meta_ref, lens_ref,
    own_hbm, far_hbm, rx_hbm, cos_hbm, sin_hbm,
    pool_hbm, pool2_hbm, got_hbm, got2_hbm,
    out_hbm, new_hbm,
    own_ref, far_ref, rx_ref, cos_ref, sin_ref, out_ref, new_ref,
    q_scr, f_scr, page_scr, mask_scr, sem,
):
    odd = par_ref[0]
    copies = fetch(
        (
            (pool_hbm, page_scr.at[0, :POOL]), (got_hbm, page_scr.at[0, POOL:ZERO_PAGE]),
            (own_hbm, own_ref), (far_hbm, far_ref), (rx_hbm, rx_ref),
            (cos_hbm, cos_ref), (sin_hbm, sin_ref),
            (pool2_hbm, page_scr.at[1, :POOL]), (got2_hbm, page_scr.at[1, POOL:ZERO_PAGE]),
        ),
        sem,
    )
    page_masks(mask_scr)
    page_scr[0, ZERO_PAGE] = jnp.zeros((16, HEAD), BF16)
    settle(copies[:2])

    def keep(g, _):
        kept = []
        for e in range(4):
            for b in range(8):
                p = 4 * g + e
                kept.append((meta_ref[TARGET + b, p], page_scr[0, lens_ref[FROM + b, p]]))
        for at, page in kept:
            new_ref[at] = page
        return 0

    lax.fori_loop(0, 32, keep, 0)
    settle(copies[2:7])
    cos, sin = cos_ref[...], sin_ref[...]

    def turn(v):
        return v * cos + pltpu.roll(v, HEAD // 2, 1) * sin

    for h in range(4):
        at = slice(h * HEAD, (h + 1) * HEAD)
        q_scr[:, at] = turn(own_ref[:, at] + rx_ref[:, at])
    kv_own = far_ref[:, 512:640] + rx_ref[:, 640:768]
    kv_oth = far_ref[:, 640:768] + rx_ref[:, 512:640]
    key = turn(jnp.where(odd == 0, kv_own, kv_oth))
    value = jnp.where(odd == 0, kv_oth, kv_own)
    f_scr[:, :HEAD] = key
    f_scr[:, HEAD : 2 * HEAD] = value
    f_scr[:, 2 * HEAD :] = jnp.where(odd == 0, key, value)

    gap = jnp.where(
        iota((256, 32), 0) // 32 == iota((256, 32), 1) // 4,
        iota((256, 32), 0) % 32 - iota((256, 32), 1) % 4,
        -1,
    )
    c32 = iota((1, 32), 1) // 4

    def edge(g, _):
        at = [8 * g + e for e in range(8)]
        lengths = [lens_ref[LENGTH, p] for p in at]
        first = [jnp.minimum(n // 16, 6) for n in lengths]
        fresh = f_scr[pl.ds(pl.multiple_of(32 * g, 32), 32), 2 * HEAD :].astype(BF16)
        start = jnp.zeros((1, 32), I32)
        for e in range(8):
            start = jnp.where(c32 == e, lengths[e] - 16 * first[e], start)
        land = jnp.where(gap == start, 1.0, 0.0).astype(BF16)
        placed = jnp.dot(land, fresh, preferred_element_type=F32).astype(BF16)
        done = []
        for e, p in enumerate(at):
            for k in range(2):
                b = first[e] + k
                lo = e * 32 + k * 16
                page = page_scr[0, meta_ref[SOURCE + b, p]] * mask_scr[lens_ref[KEPT + b, p]]
                done.append((meta_ref[TARGET + b, p], page + placed[lo : lo + 16]))
        for to, page in done:
            new_ref[to] = page
        return 0

    scale = 1.0 / math.sqrt(HEAD)
    row2 = (iota((32, HEAD), 0) % 8) // 4
    lane32 = iota((32, HEAD), 1)
    col_a = jnp.where(row2 == 0, lane32, HEAD)
    col_b = jnp.where(row2 == 1, lane32, HEAD)
    row = iota((HEAD, HEAD), 0)
    col_new = iota((HEAD, HEAD), 1) - (row // 32) * 8 - (row % 8) // 4 * 4
    contract = (((1,), (1,)), ((), ()))

    def mix(g, _):
        q32 = q_scr[pl.ds(pl.multiple_of(32 * g, 32), 32), :]
        q = jnp.concatenate(
            [
                q32[8 * k : 8 * k + 8, h * HEAD : (h + 1) * HEAD]
                for k in range(GROUP)
                for h in range(4)
            ],
            axis=0,
        ).astype(BF16)
        block = pl.ds(pl.multiple_of((g // 4) * HEAD, HEAD), HEAD)
        fresh_k = f_scr[block, :HEAD].astype(BF16)
        fresh_v = f_scr[block, HEAD : 2 * HEAD].astype(BF16)
        new = lax.dot_general(q, fresh_k, contract, preferred_element_type=F32)
        rel = col_new - 32 * (g % 4)
        new = jnp.where((rel >= 0) & (rel <= row % 4), new, -1e30)
        lengths = [lens_ref[LENGTH, 8 * g + e] for e in range(8)]
        index = [meta_ref[SOURCE + b, 8 * g + e] for e in range(8) for b in range(8)]
        old_a, old_b = [], []
        for k in range(GROUP):
            keys = jnp.concatenate([page_scr[odd, j] for j in index[16 * k : 16 * k + 16]], axis=0)
            old = lax.dot_general(
                q[32 * k : 32 * k + 32], keys, contract, preferred_element_type=F32
            )
            old_a.append(jnp.where(col_a < lengths[2 * k], old[:, :HEAD], -1e30))
            old_b.append(jnp.where(col_b < lengths[2 * k + 1], old[:, HEAD:], -1e30))
        old_a, old_b = jnp.concatenate(old_a, axis=0), jnp.concatenate(old_b, axis=0)
        top = jnp.max(jnp.maximum(jnp.maximum(old_a, old_b), new), axis=1, keepdims=True)
        old_a, old_b, new = (jnp.exp((v - top) * scale) for v in (old_a, old_b, new))
        part = 1.0 / jnp.sum(old_a + old_b + new, axis=1, keepdims=True)
        old = jnp.concatenate([old_a * part, old_b * part], axis=1).astype(BF16)
        mixed = jnp.dot((new * part).astype(BF16), fresh_v, preferred_element_type=F32)
        old_mixed = []
        for k in range(GROUP):
            values = jnp.concatenate(
                [page_scr[1 - odd, j] for j in index[16 * k : 16 * k + 16]], axis=0
            )
            old_mixed.append(
                jnp.dot(old[32 * k : 32 * k + 32], values, preferred_element_type=F32)
            )
        mixed = (mixed + jnp.concatenate(old_mixed, axis=0)).astype(BF16)
        for k in range(GROUP):
            for e in range(2):
                slot = meta_ref[SLOT, 8 * g + 2 * k + e]
                for h in range(4):
                    lo = k * 32 + h * 8 + e * 4
                    out_ref[slot, :, h * HEAD : (h + 1) * HEAD] = mixed[lo : lo + 4]
        return 0

    lax.fori_loop(0, 16, edge, 0)
    stores = fetch(((new_ref, new_hbm),), sem)
    settle(copies[7:])
    lax.fori_loop(0, 16, mix, 0)
    settle(stores + fetch(((out_ref, out_hbm),), sem, 1))


def attend(parity, meta, lens, own, far, rx, cos, sin, pool, pool2, got, got2):
    outs = (sds((128, 4, 512), BF16), sds(pool.shape, BF16))
    return pl.pallas_call(
        attend_kernel,
        out_shape=outs,
        in_specs=[sspec()] * 3 + [hspec()] * 9,
        out_specs=(hspec(), hspec()),
        scratch_shapes=[pltpu.VMEM(a.shape, a.dtype) for a in (own, far, rx, cos, sin, *outs)]
        + [
            pltpu.VMEM((512, 512), F32),
            pltpu.VMEM((512, 3 * HEAD), F32),
            pltpu.VMEM((2, ZERO_PAGE + 1, 16, HEAD), BF16),
            pltpu.VMEM((17, 16, HEAD), BF16),
            pltpu.SemaphoreType.DMA((9,)),
        ],
        compiler_params=params(),
        name="attend",
    )(parity, meta, lens, own, far, rx, cos, sin, pool, pool2, got, got2)


def body(
    tokens,
    query_weight_matrix,
    key_value_weight,
    adapter_down_factors,
    adapter_up_query,
    adapter_up_key_value,
    storage_slot_adapter,
    slot_request_adapter,
    migration,
    lengths,
    previous_block_table,
    moved_block_table,
    paged_cache_pool,
):
    r = lax.axis_index("rep").astype(I32)
    t = lax.axis_index("tp").astype(I32)
    core = t % 2

    def other_core(a):
        return lax.ppermute(a, "tp", [(i, i ^ 1) for i in range(16)])

    def other_x(a):
        return lax.ppermute(a, "tp", [(i, i ^ 2) for i in range(16)])

    def along_y(a, d):
        return lax.ppermute(a, "tp", [(i, (i + 4 * d) % 16) for i in range(16)])

    def swap_rep(a):
        return lax.all_to_all(a, "rep", split_axis=0, concat_axis=0, tiled=True)

    send, own, cand, meta = plan(
        r.reshape(1), migration.reshape(8, 128), slot_request_adapter.reshape(8, 128),
        storage_slot_adapter.reshape(1, 64), lengths.reshape(1, 128),
        previous_block_table.T, moved_block_table.T, tokens.reshape(512, 512),
    )
    packed = pack_adapters(meta, adapter_down_factors, adapter_up_query, adapter_up_key_value)
    pool2 = other_core(paged_cache_pool)
    vq, vk = other_core(query_weight_matrix), other_core(key_value_weight)
    leaving = pack_cache(meta, paged_cache_pool)
    x, length, lens = join(own, swap_rep(send), meta, packed, leaving, pool2)
    far = swap_rep(packed)

    hi = (t // 2) % 2
    y = t // 4

    def js(*blocks):
        at = [(((y + dy) % 4) * 2 + (hi ^ dx)) * 2 + core for dy, dx in blocks]
        return jnp.stack(at).astype(I32)

    weights = (query_weight_matrix, key_value_weight, vq, vk)
    one = core.reshape(1)
    xh = other_x(x)
    yp = along_y(x, 1)
    ym = along_y(x, -1)
    full = (0, 512)
    up, dn = slices(
        ((0, (0, 512), 0, 0), (1, (0, 256), 0, 512), (0, (0, 512), 1, 0), (2, (256, 512), 1, 512)),
        (768, 768), (xh, yp, ym), (vq, vk),
    )
    leaving, far, _ = lax.optimization_barrier((leaving, far, up))
    got = swap_rep(leaving)
    got2 = other_core(got)
    up, dn = along_y(up, 1), along_y(dn, -1)
    acc = matmul(
        js((0, 0), (0, 1), (3, 0), (1, 0)),
        tuple(((i, *full),) for i in range(4)),
        (x, xh, yp, ym), weights,
    )
    keep, give = down_product(one, x, adapter_down_factors, far, cand)
    up2, dn2 = slices(
        ((0, (0, 256), 0, 0), (1, (256, 512), 1, 0)), (256, 256), (up, dn), (acc[0], keep)
    )
    last = (along_y(up2, 1), along_y(dn2, -1))
    total = keep + other_core(give)
    total = total + other_x(total)
    total = (total + along_y(total, 2)) + (along_y(total, 1) + along_y(total, -1))
    total = total.astype(BF16)
    delta, cos, sin = up_product(
        one, total, other_core(total), far, cand, adapter_up_query, adapter_up_key_value, length,
        acc[0],
    )
    acc_own, acc_far = matmul(
        js((3, 1), (1, 1), (2, 0), (2, 1)),
        (
            ((0, *full),), ((1, *full),), ((0, 512, 768), (1, 512, 768)),
            ((2, 0, 256), (3, 0, 256)),
        ),
        (up, dn, *last), weights, (*acc, delta),
    )
    rx = other_core(acc_far)
    return attend(
        one, meta, lens, acc_own, acc_far, rx, cos, sin, paged_cache_pool, pool2, got, got2
    )


def solution(mesh):
    in_specs = (
        P("rep", None, "tp"),
        P(None, "tp"),
        P(None, "tp"),
        P("rep", "tp", None),
        P("rep", None, "tp"),
        P("rep", None, "tp"),
        P(),
        P(),
        P(),
        P("rep"),
        P("rep", None),
        P("rep", None),
        P("rep", None, "tp"),
    )
    out_specs = (P("rep", None, "tp"), P("rep", None, "tp"))
    return jax.shard_map(body, mesh=mesh, in_specs=in_specs, out_specs=out_specs, check_vma=False)
```

```python
import functools
import math

import jax
import jax.numpy as jnp
import ml_dtypes
import numpy as np
from jax import lax
from jax.experimental import pallas as pl
from jax.experimental.pallas import tpu as pltpu
from jax.sharding import PartitionSpec as P

HEAD = 128
THETA = 500000.0
MIB = 1 << 20
VMEM_MIB = 60
POOL = 1024
ZERO_PAGE = POOL + 512

SLOT, PICK, SOURCE, TARGET, LEAVE = 0, 3, 8, 16, 24
KEPT, LENGTH, FROM = 0, 8, 16

F32 = jnp.float32
BF16 = jnp.bfloat16
I32 = jnp.int32


def iota(shape, axis):
    return lax.broadcasted_iota(I32, shape, axis)


def col_to_row(col):
    n = col.shape[0]
    return jnp.sum(jnp.where(iota((n, n), 0) == iota((n, n), 1), col, 0), axis=0, keepdims=True)


def row_to_col(row, n, stretch=1):
    w = row.shape[1]
    return jnp.sum(
        jnp.where(iota((n, w), 1) == iota((n, w), 0) // stretch, row, 0), axis=1, keepdims=True
    )


def below(mask):
    n = mask.shape[1]
    tri = (iota((n, n), 0) < iota((n, n), 1)).astype(BF16)
    return jnp.dot(mask.astype(BF16), tri, preferred_element_type=F32).astype(I32)


def plan_kernel(
    me_ref, mig_hbm, sra_hbm, ssa_hbm, len_hbm, prev_hbm, moved_hbm, tok_hbm,
    send_hbm, own_hbm, cand_hbm, meta_hbm,
    mig_ref, sra_ref, ssa_ref, len_ref, prev_ref, moved_ref, tok_ref, send_ref, own_ref, cand_ref, meta_ref, sem,
):
    loads = fetch(
        (
            (mig_hbm, mig_ref), (sra_hbm, sra_ref), (ssa_hbm, ssa_ref), (len_hbm, len_ref),
            (prev_hbm, prev_ref), (moved_hbm, moved_ref), (tok_hbm, tok_ref),
        ),
        sem,
    )
    settle(loads[:6])
    r = me_ref[0]
    groups, per = mig_ref.shape
    half = per // 2
    mig = mig_ref[...]
    grp, loc = mig // per, mig % per
    drow = iota((groups, per), 0)
    out_mask = ((grp == r) & (drow != r)).astype(I32)
    mine = jnp.sum(jnp.where(drow == r, mig, 0), axis=0, keepdims=True)
    g_in, loc_in = mine // per, mine % per
    in_mask = (g_in == drow).astype(I32)
    ranks = below(jnp.concatenate([out_mask, in_mask], axis=0))
    out_rank, in_ranks = ranks[:groups], ranks[groups:]
    in_rank = jnp.sum(in_mask * in_ranks, axis=0, keepdims=True)
    stay = g_in == r

    parts = []
    for d in range(groups):
        hit = (out_mask[d : d + 1] == 1) & (out_rank[d : d + 1] == iota((groups, per), 0))
        parts.append(jnp.sum(jnp.where(hit, loc[d : d + 1] + 1, 0), axis=1, keepdims=True))
    src_col = jnp.concatenate(parts, axis=0) - 1
    src_row = col_to_row(src_col)

    count = jnp.sum(jnp.where(drow == r, 0, in_mask), axis=1, keepdims=True)
    lane_u = iota((groups, half), 1)
    count_u = jnp.sum(jnp.where(iota((groups, half), 0) == lane_u // groups, count, 0), axis=0, keepdims=True)
    free = (lane_u[:1] % groups >= count_u).astype(I32)
    free_rank = jnp.where(free == 1, below(free), -1)
    free_col = row_to_col(free_rank, half)
    extra = jnp.sum(
        jnp.where(free_col == in_rank - half, iota((half, per), 0), 0), axis=0, keepdims=True
    )
    place = jnp.where(
        stay, jnp.where(in_rank < half, in_rank, half + extra), half + groups * g_in + in_rank
    )
    sel = place == iota((per, per), 0)

    def placed(row):
        return jnp.sum(jnp.where(sel, row, 0), axis=1, keepdims=True)

    slot_row = col_to_row(placed(iota((1, per), 1)))
    loc_row = col_to_row(placed(jnp.where(stay, loc_in, -1)))

    drow_sra = iota(sra_ref.shape, 0)
    sra = sra_ref[...]
    wanted = jnp.sum(jnp.where(drow_sra == r, sra, 0), axis=0, keepdims=True)
    ssa_col = row_to_col(ssa_ref[...], half)
    store = jnp.sum(jnp.where(ssa_col == wanted, iota((half, per), 0), 0), axis=0, keepdims=True)
    cand = jnp.where(store // groups == r, store % groups, groups + store // groups)
    cand_row = col_to_row(placed(cand))
    rows = per * 4
    cand_ref[...] = jnp.broadcast_to(row_to_col(cand_row, rows, 4), (rows, HEAD)).astype(BF16)
    picks = jnp.zeros((groups, 1), I32)
    lane_s = iota((1, half), 1)
    for i in range(groups):
        name = jnp.sum(jnp.where(lane_s == r * groups + i, ssa_ref[...], 0), axis=1, keepdims=True)
        used = jnp.max((sra == name).astype(I32), axis=1, keepdims=True)
        picks = jnp.maximum(picks, used * i)
    pick_row = jnp.sum(
        jnp.where(iota((groups, per), 0) == iota((groups, per), 1), picks, 0), axis=0, keepdims=True
    )

    len_col = jnp.broadcast_to(row_to_col(len_ref[...], rows, 4), (rows, HEAD))
    settle(loads[6:])
    tok = jnp.concatenate([tok_ref[...], len_col.astype(F32).astype(BF16)], axis=1)

    def rows_of(row, n):
        base = row_to_col(row, n, 4)
        at = 4 * base + iota((n, 1), 0) % 4
        pick = (jnp.broadcast_to(at, (n, rows)) == iota((n, rows), 1)) & (base >= 0)
        return jnp.dot(
            jnp.where(pick, 1.0, 0.0).astype(BF16), tok, preferred_element_type=F32
        ).astype(BF16)

    send_ref[...] = rows_of(src_row, rows // 2)
    stores = fetch(((send_ref, send_hbm),), sem)
    own_ref[...] = rows_of(loc_row, rows)
    stores += fetch(((own_ref, own_hbm),), sem, 1)
    src_wide = jnp.sum(
        jnp.where(iota((half, per), 0) == iota((half, per), 1), src_col, 0), axis=0, keepdims=True
    )
    def looked_up(table, row):
        pick = jnp.where(row == iota((per, per), 0), 1.0, 0.0).astype(BF16)
        parts = jnp.concatenate([table // 32, table % 32], axis=0).astype(F32).astype(BF16)
        found = jnp.dot(parts, pick, preferred_element_type=F32).astype(I32)
        return found[:8] * 32 + found[8:]

    prev, moved = prev_ref[...], moved_ref[...]
    lane8, row8 = iota((8, per), 1), iota((8, per), 0)
    source = jnp.where(loc_row >= 0, looked_up(prev, loc_row), POOL + (lane8 - half) * 8 + row8)
    target = looked_up(moved, slot_row)
    leave = looked_up(prev, src_wide)
    zero = jnp.zeros((groups - 4, per), I32)
    meta_ref[...] = jnp.concatenate(
        [slot_row, loc_row, src_wide, pick_row, zero, source, target, leave], axis=0
    )
    stores += fetch(((cand_ref, cand_hbm), (meta_ref, meta_hbm)), sem, 2)
    settle(stores)


def hspec():
    return pl.BlockSpec(memory_space=pltpu.HBM)


def fetch(pairs, sem, at=0):
    copies = [pltpu.make_async_copy(a, b, sem.at[at + n]) for n, (a, b) in enumerate(pairs)]
    for c in copies:
        c.start()
    return copies


def settle(copies):
    for c in copies:
        c.wait()


def sspec():
    return pl.BlockSpec(memory_space=pltpu.SMEM)


def params():
    return pltpu.CompilerParams(vmem_limit_bytes=VMEM_MIB * MIB)


def sds(shape, dtype):
    return jax.ShapeDtypeStruct(shape, dtype)


def plan(me, mig, sra, ssa, lengths, prev, moved, tok):
    rows = tok.shape[0]
    ins = (mig, sra, ssa, lengths, prev, moved, tok)
    outs = (
        sds((rows // 2, 640), BF16),
        sds((rows, 640), BF16),
        sds((rows, HEAD), BF16),
        sds((32, HEAD), I32),
    )
    return pl.pallas_call(
        plan_kernel,
        out_shape=outs,
        in_specs=[sspec()] + [hspec()] * 7,
        out_specs=(hspec(),) * 4,
        scratch_shapes=[pltpu.VMEM(a.shape, a.dtype) for a in ins + outs]
        + [pltpu.SemaphoreType.DMA((7,))],
        compiler_params=params(),
        name="plan",
    )(me, *ins)


def pack_kernel(
    meta_ref, down_hbm, q_hbm, k_hbm, pool_hbm, down_out, rest_out,
    down_ref, q_ref, k_ref, pool_ref, rest_ref, sem, pool_sem,
):
    pairs = [(down_hbm.at[meta_ref[PICK, d]], down_ref.at[d]) for d in range(8)]
    loads = fetch(pairs, sem)
    later = fetch(((pool_hbm, pool_ref), (q_hbm, q_ref), (k_hbm, k_ref)), pool_sem)
    settle(loads)
    stores = fetch(((down_ref, down_out),), sem)
    settle(later)
    for d in range(8):
        i = meta_ref[PICK, d]
        q = q_ref[i]
        for h in range(4):
            rest_ref[d, 64 + 4 * h : 68 + 4 * h] = q[:, h * HEAD : (h + 1) * HEAD].reshape(4, 16, HEAD)
        rest_ref[d, 80:84] = k_ref[i].reshape(4, 16, HEAD)

    def some(g, _):
        pages = [pool_ref[meta_ref[LEAVE + b, 4 * g + e]] for e in range(4) for b in range(8)]
        for n, page in enumerate(pages):
            rest_ref[g // 2, (g % 2) * 32 + n] = page
        return 0

    lax.fori_loop(0, 16, some, 0)
    settle(stores + fetch(((rest_ref, rest_out),), pool_sem))


def pack(meta, down, up_q, up_kv, pool):
    rest = sds((8, 84, 16, HEAD), BF16)
    return pl.pallas_call(
        pack_kernel,
        out_shape=(sds(down.shape, BF16), rest),
        in_specs=[sspec()] + [hspec()] * 4,
        out_specs=(hspec(), hspec()),
        scratch_shapes=[pltpu.VMEM(a.shape, BF16) for a in (down, up_q, up_kv, pool, rest)]
        + [pltpu.SemaphoreType.DMA((8,)), pltpu.SemaphoreType.DMA((3,))],
        compiler_params=params(),
        name="pack",
    )(meta, down, up_q, up_kv, pool)


def join_kernel(
    own_hbm, got_hbm, meta_hbm, after_ref, after2_ref, x_hbm, len_hbm, lens_hbm,
    own_ref, got_ref, meta_ref, x_ref, len_ref, lens_ref, sem,
):
    settle(fetch(((own_hbm, own_ref), (got_hbm, got_ref), (meta_hbm, meta_ref)), sem))
    rows = x_ref.shape[0]
    x_ref[: rows // 2] = own_ref[: rows // 2, :512]
    x_ref[rows // 2 :] = own_ref[rows // 2 :, :512] + got_ref[:, :512]
    store = fetch(((x_ref, x_hbm),), sem)
    length = jnp.concatenate(
        [own_ref[: rows // 2, 512:], own_ref[rows // 2 :, 512:] + got_ref[:, 512:]], axis=0
    ).astype(F32)
    len_ref[...] = length
    row = jnp.sum(
        jnp.where(iota((rows, HEAD), 0) == 4 * iota((rows, HEAD), 1), length, 0.0),
        axis=0,
        keepdims=True,
    ).astype(I32)
    kept = jnp.clip(row - 16 * iota((8, HEAD), 0), 0, 16)
    lens_ref[KEPT : KEPT + 8] = kept
    lens_ref[LENGTH : LENGTH + 8] = jnp.broadcast_to(row, (8, HEAD))
    lens_ref[FROM : FROM + 8] = jnp.where(kept > 0, meta_ref[SOURCE : SOURCE + 8], ZERO_PAGE)
    settle(store + fetch(((len_ref, len_hbm), (lens_ref, lens_hbm)), sem, 1))


def join(own, got, meta, *after):
    rows = own.shape[0]
    return pl.pallas_call(
        join_kernel,
        out_shape=(sds((rows, 512), BF16), sds((rows, HEAD), F32), sds((24, HEAD), I32)),
        in_specs=[hspec()] * 5,
        out_specs=(hspec(),) * 3,
        scratch_shapes=[
            pltpu.VMEM(own.shape, BF16),
            pltpu.VMEM(got.shape, BF16),
            pltpu.VMEM(meta.shape, I32),
            pltpu.VMEM((rows, 512), BF16),
            pltpu.VMEM((rows, HEAD), F32),
            pltpu.VMEM((24, HEAD), I32),
            pltpu.SemaphoreType.DMA((3,)),
        ],
        compiler_params=params(),
        name="join",
    )(own, got, meta, *after)


def slices_kernel(moves, n, *refs):
    outs = len({m[2] for m in moves})
    ins, dst = refs[:n], refs[-1 - 2 * outs : -1 - outs]
    tmp, sem = refs[-1 - outs : -1], refs[-1]
    loads = fetch(
        [(ins[i].at[lo:hi], tmp[o].at[at : at + hi - lo]) for i, (lo, hi), o, at in moves], sem
    )
    settle(loads)
    settle(fetch([(t, d) for t, d in zip(tmp, dst)], sem))


def slices(moves, rows, arrays, after):
    shapes = [(n, 512) for n in rows]
    return pl.pallas_call(
        functools.partial(slices_kernel, moves, len(arrays)),
        out_shape=tuple(sds(s, BF16) for s in shapes),
        in_specs=[hspec()] * (len(arrays) + len(after)),
        out_specs=(hspec(),) * len(rows),
        scratch_shapes=[pltpu.VMEM(s, BF16) for s in shapes]
        + [pltpu.SemaphoreType.DMA((len(moves),))],
        compiler_params=params(),
        name="slices",
    )(*arrays, *after)


COLUMNS = {"far": ((2, 512, 0), (1, HEAD, 512), (3, HEAD, 640)), "own": ((0, 512, 0),)}
WIDTH = {"far": 768, "own": 512}


def matmul_kernel(blocks, offsets, chunk, n, parts, extra, after, at_ref, *refs):
    np_, nb = len(parts), len(blocks)
    xs, refs = refs[:n], refs[n:]
    weights, refs = refs[:4], refs[4:]
    adds, refs = refs[: extra * np_], refs[extra * np_ + after :]
    outs, refs = refs[:np_], refs[np_:]
    bufs, refs = refs[:np_], refs[np_:]
    add, refs = refs[: extra * np_], refs[extra * np_ :]
    res, refs = refs[:np_], refs[np_:]
    x_ref, x_sem, sem, add_sem, out_sem = refs
    y, hi, core = at_ref[0] // 4, (at_ref[0] // 2) % 2, at_ref[0] % 2
    place = [(((y + dy) % 4) * 2 + (hi + dx) % 2) * 2 + core for dy, dx in offsets]
    x_loads, w_loads = [], {}
    for k, cut in enumerate(blocks):
        row = 0
        for j, (i, lo, hi) in enumerate(cut):
            to = x_ref.at[row : row + hi - lo, k * 512 : (k + 1) * 512]
            x_loads.append((k, pltpu.make_async_copy(xs[i].at[lo:hi], to, x_sem.at[k, j])))
            row += hi - lo
    for o, part in enumerate(parts):
        for k in range(nb):
            at = pl.ds(pl.multiple_of(place[k] * 512, 512), 512)
            w_loads[o, k] = [
                pltpu.make_async_copy(
                    weights[w].at[at],
                    bufs[o].at[k * 512 : (k + 1) * 512, lo : lo + width],
                    sem.at[k, w],
                )
                for w, width, lo in COLUMNS[part]
            ]
    for k in range(nb):
        for c in [c for at, c in x_loads if at == k] + w_loads[0, k]:
            c.start()
    add_loads = fetch(list(zip(adds, add)), add_sem)
    for o in range(1, np_):
        for k in range(nb):
            for c in w_loads[o, k]:
                c.start()
    stores = []
    for o in range(np_):
        for c in range(0, nb, chunk):
            for k in range(c, c + chunk):
                if o == 0:
                    settle([copy for at, copy in x_loads if at == k])
                settle(w_loads[o, k])
            at = slice(c * 512, (c + chunk) * 512)
            y = jnp.dot(x_ref[:, at], bufs[o][at], preferred_element_type=F32)
            if c == 0:
                settle(add_loads[o * extra : (o + 1) * extra])
                for a in add[o * extra : (o + 1) * extra]:
                    y = y + a[...]
                res[o][...] = y
            else:
                res[o][...] += y
        stores += fetch(((res[o], outs[o]),), out_sem, o)
    settle(stores)


def matmul(parts, at, offsets, blocks, xs, weights, adds=(), after=(), chunk=4):
    nb = len(blocks)
    outs = tuple(sds((512, WIDTH[p]), F32) for p in parts)
    flat = tuple(a[o] for o in range(len(parts)) for a in adds)
    return pl.pallas_call(
        functools.partial(
            matmul_kernel, blocks, offsets, min(chunk, nb), len(xs), parts, len(adds), len(after)
        ),
        out_shape=outs,
        in_specs=[sspec()] + [hspec()] * (len(xs) + 4 + len(flat) + len(after)),
        out_specs=(hspec(),) * len(parts),
        scratch_shapes=[pltpu.VMEM((nb * 512, WIDTH[p]), BF16) for p in parts]
        + [pltpu.VMEM(a.shape, a.dtype) for a in (*flat, *outs)]
        + [
            pltpu.VMEM((512, nb * 512), BF16),
            pltpu.SemaphoreType.DMA((nb, 2)),
            pltpu.SemaphoreType.DMA((nb, 4)),
            pltpu.SemaphoreType.DMA((max(1, len(flat)),)),
            pltpu.SemaphoreType.DMA((len(parts),)),
        ],
        compiler_params=params(),
        name="matmul_" + "_".join(parts),
    )(at, *xs, *weights, *flat, *after)


def down_kernel(
    core_ref, x_hbm, here_hbm, far_hbm, cand_hbm, keep_hbm, give_hbm,
    x_ref, here_ref, far_ref, cand_ref, out_ref, sem,
):
    loads = fetch(
        ((x_hbm, x_ref), (here_hbm, here_ref), (cand_hbm, cand_ref), (far_hbm, far_ref)),
        sem,
    )
    settle(loads[:3])
    x = x_ref[...]
    cand = cand_ref[...].astype(F32)
    acc = None
    for a in range(0, 16, 2):
        if a == 8:
            settle(loads[3:])
        ref = here_ref if a < 8 else far_ref
        b = a % 8
        w = jnp.concatenate([ref[b], ref[b + 1]], axis=1)
        y = jnp.dot(x, w, preferred_element_type=F32)
        y = jnp.where(cand == float(a), y[:, :HEAD], jnp.where(cand == float(a + 1), y[:, HEAD:], 0.0))
        acc = y if acc is None else acc + y
    out_ref[...] = acc
    half = out_ref.shape[0] // 2
    mine = pl.ds(pl.multiple_of(core_ref[0] * half, half), half)
    other = pl.ds(pl.multiple_of((1 - core_ref[0]) * half, half), half)
    settle(fetch(((out_ref.at[mine], keep_hbm), (out_ref.at[other], give_hbm)), sem))


def down_product(core, x, here, far, cand):
    rows = x.shape[0]
    return pl.pallas_call(
        down_kernel,
        out_shape=(sds((rows // 2, HEAD), F32),) * 2,
        in_specs=[sspec()] + [hspec()] * 4,
        out_specs=(hspec(), hspec()),
        scratch_shapes=[
            pltpu.VMEM(x.shape, BF16),
            pltpu.VMEM(here.shape, BF16),
            pltpu.VMEM(here.shape, BF16),
            pltpu.VMEM(cand.shape, BF16),
            pltpu.VMEM((rows, HEAD), F32),
            pltpu.SemaphoreType.DMA((4,)),
        ],
        compiler_params=params(),
        name="down_product",
    )(core, x, here, far, cand)


def turn_table():
    frequency = np.float32(THETA) ** (-(np.arange(HEAD // 2, dtype=np.float32) * 2.0 / HEAD))
    angles = np.arange(HEAD, dtype=np.float32)[:, None] * frequency.astype(np.float32)
    cos, sin = np.cos(angles.astype(np.float64)), np.sin(angles.astype(np.float64))
    rest = np.concatenate([cos, cos, -sin, sin], axis=1).astype(np.float32)
    terms = []
    for _ in range(3):
        terms.append(rest.astype(ml_dtypes.bfloat16))
        rest = rest - terms[-1].astype(np.float32)
    return np.concatenate(terms, axis=1)


def up_kernel(
    core_ref, mine_hbm, other_hbm, far_hbm, cand_hbm, q_hbm, k_hbm, len_hbm, table_hbm, acc_hbm,
    out_hbm, kv_hbm, cos_hbm, sin_hbm,
    down_ref, far, cand_ref, q_here, k_here, len_ref, table_ref, acc_ref,
    out_ref, kv_ref, cos_ref, sin_ref, sem,
):
    half = mine_hbm.shape[0]
    mine = pl.ds(pl.multiple_of(core_ref[0] * half, half), half)
    other = pl.ds(pl.multiple_of((1 - core_ref[0]) * half, half), half)
    settle(
        fetch(
            (
                (mine_hbm, down_ref.at[mine]), (other_hbm, down_ref.at[other]),
                (far_hbm.at[:, 64:], far), (cand_hbm, cand_ref), (q_hbm, q_here),
                (k_hbm, k_here), (len_hbm, len_ref), (table_hbm, table_ref), (acc_hbm, acc_ref),
            ),
            sem,
        )
    )
    down = down_ref[...].astype(F32)
    cand = cand_ref[...].astype(F32)
    rows = down.shape[0]
    lane = iota((rows, HEAD), 1)
    upper = lane >= HEAD // 2
    other = pltpu.roll(down, HEAD // 2, 1)
    down_q = jnp.where(upper, other, down)
    down_k = jnp.where(upper, down, other)
    shift = jnp.where(upper, 1.0, 0.0)

    def spread(v):
        return jnp.concatenate(
            [jnp.where(cand == shift + float(2 * i), v, 0.0).astype(BF16) for i in range(8)], axis=1
        )

    sq, sk = spread(down_q), spread(down_k)
    q_all, k_all = q_here[...].reshape(512, 512), k_here[...].reshape(512, HEAD)

    def far_part(lo):
        return jnp.concatenate(
            [far[a, lo // 16 : lo // 16 + 4].reshape(64, HEAD) for a in range(8)], axis=0
        )

    w = [
        jnp.concatenate([q_all[:, h * HEAD : (h + 1) * HEAD], far_part(64 * h)], axis=0)
        for h in range(4)
    ]
    for h in (0, 2):
        at = slice(h * HEAD, (h + 2) * HEAD)
        out_ref[:, at] = acc_ref[:, at] + jnp.dot(
            sq, jnp.concatenate([w[h], w[h + 1]], axis=1), preferred_element_type=F32
        )
    kv_ref[...] = jnp.dot(
        sk, jnp.concatenate([k_all, far_part(256)], axis=0), preferred_element_type=F32
    )
    position = len_ref[...].astype(I32) + iota((rows, HEAD), 0) % 4
    pick = jnp.where(position == lane, 1.0, 0.0).astype(BF16)
    turns = jnp.dot(pick, table_ref[...], preferred_element_type=F32)
    turns = turns[:, :256] + turns[:, 256:512] + turns[:, 512:]
    cos_ref[...] = turns[:, :HEAD]
    sin_ref[...] = turns[:, HEAD:]
    settle(
        fetch(
            ((out_ref, out_hbm), (kv_ref, kv_hbm), (cos_ref, cos_hbm), (sin_ref, sin_hbm)), sem
        )
    )


def up_product(core, mine, other, far, cand, up_q, up_kv, length, acc):
    rows = cand.shape[0]
    ins = (cand, up_q, up_kv, length, jnp.asarray(turn_table()), acc)
    outs = (sds((rows, 512), F32),) + (sds((rows, HEAD), F32),) * 3
    return pl.pallas_call(
        up_kernel,
        out_shape=outs,
        in_specs=[sspec()] + [hspec()] * 9,
        out_specs=(hspec(),) * 4,
        scratch_shapes=[pltpu.VMEM((rows, HEAD), BF16), pltpu.VMEM((8, 20, 16, HEAD), BF16)]
        + [pltpu.VMEM(a.shape, a.dtype) for a in ins + outs]
        + [pltpu.SemaphoreType.DMA((9,))],
        compiler_params=params(),
        name="up_product",
    )(core, mine, other, far, *ins)


GROUP = 4


def page_masks(mask_scr):
    for d in range(17):
        mask_scr[d] = jnp.where(iota((16, HEAD), 0) < d, 1.0, 0.0).astype(BF16)


def attend_kernel(
    par_ref, meta_ref, lens_ref,
    own_hbm, far_hbm, rx_hbm, kv_hbm, kv2_hbm, cos_hbm, sin_hbm,
    pool_hbm, pool2_hbm, got_hbm, got2_hbm,
    out_hbm, new_hbm,
    own_ref, far_ref, rx_ref, kv_ref, kv2_ref, cos_ref, sin_ref, out_ref, new_ref,
    q_scr, f_scr, page_scr, mask_scr, sem,
):
    odd = par_ref[0]
    def pages_from(i, pool, got):
        return [(pool, page_scr.at[i, :POOL])] + [
            (got.at[g, :64], page_scr.at[i, POOL + 64 * g : POOL + 64 * g + 64]) for g in range(8)
        ]

    copies = fetch(
        (
            *pages_from(0, pool_hbm, got_hbm),
            (far_hbm, far_ref), (rx_hbm, rx_ref), (kv_hbm, kv_ref), (kv2_hbm, kv2_ref),
            (cos_hbm, cos_ref), (sin_hbm, sin_ref), (own_hbm, own_ref),
            *pages_from(1, pool2_hbm, got2_hbm),
        ),
        sem,
    )
    page_masks(mask_scr)
    page_scr[0, ZERO_PAGE] = jnp.zeros((16, HEAD), BF16)
    settle(copies[:9])

    def keep(g, _):
        kept = []
        for e in range(4):
            for b in range(8):
                p = 4 * g + e
                kept.append((meta_ref[TARGET + b, p], page_scr[0, lens_ref[FROM + b, p]]))
        for at, page in kept:
            new_ref[at] = page
        return 0

    lax.fori_loop(0, 32, keep, 0)
    settle(copies[9:16])
    cos, sin = cos_ref[...], sin_ref[...]

    def turn(v):
        return v * cos + pltpu.roll(v, HEAD // 2, 1) * sin

    for h in range(4):
        at = slice(h * HEAD, (h + 1) * HEAD)
        q_scr[:, at] = turn(own_ref[:, at] + rx_ref[:, at])
    kv_own = far_ref[:, 512:640] + rx_ref[:, 640:768] + kv_ref[...]
    kv_oth = far_ref[:, 640:768] + rx_ref[:, 512:640] + kv2_ref[...]
    key = turn(jnp.where(odd == 0, kv_own, kv_oth))
    value = jnp.where(odd == 0, kv_oth, kv_own)
    f_scr[:, :HEAD] = key
    f_scr[:, HEAD : 2 * HEAD] = value
    f_scr[:, 2 * HEAD :] = jnp.where(odd == 0, key, value)

    gap = jnp.where(
        iota((256, 32), 0) // 32 == iota((256, 32), 1) // 4,
        iota((256, 32), 0) % 32 - iota((256, 32), 1) % 4,
        -1,
    )
    c32 = iota((1, 32), 1) // 4

    def edge(g, _):
        at = [8 * g + e for e in range(8)]
        lengths = [lens_ref[LENGTH, p] for p in at]
        first = [jnp.minimum(n // 16, 6) for n in lengths]
        fresh = f_scr[pl.ds(pl.multiple_of(32 * g, 32), 32), 2 * HEAD :].astype(BF16)
        start = jnp.zeros((1, 32), I32)
        for e in range(8):
            start = jnp.where(c32 == e, lengths[e] - 16 * first[e], start)
        land = jnp.where(gap == start, 1.0, 0.0).astype(BF16)
        placed = jnp.dot(land, fresh, preferred_element_type=F32).astype(BF16)
        done = []
        for e, p in enumerate(at):
            for k in range(2):
                b = first[e] + k
                lo = e * 32 + k * 16
                page = page_scr[0, meta_ref[SOURCE + b, p]] * mask_scr[lens_ref[KEPT + b, p]]
                done.append((meta_ref[TARGET + b, p], page + placed[lo : lo + 16]))
        for to, page in done:
            new_ref[to] = page
        return 0

    scale = 1.0 / math.sqrt(HEAD)
    row2 = (iota((32, HEAD), 0) % 8) // 4
    lane32 = iota((32, HEAD), 1)
    col_a = jnp.where(row2 == 0, lane32, HEAD)
    col_b = jnp.where(row2 == 1, lane32, HEAD)
    row = iota((HEAD, HEAD), 0)
    col_new = iota((HEAD, HEAD), 1) - (row // 32) * 8 - (row % 8) // 4 * 4
    contract = (((1,), (1,)), ((), ()))

    def mixed_rows(g):
        q32 = q_scr[pl.ds(pl.multiple_of(32 * g, 32), 32), :]
        q = jnp.concatenate(
            [
                q32[8 * k : 8 * k + 8, h * HEAD : (h + 1) * HEAD]
                for k in range(GROUP)
                for h in range(4)
            ],
            axis=0,
        ).astype(BF16)
        block = pl.ds(pl.multiple_of((g // 4) * HEAD, HEAD), HEAD)
        fresh_k = f_scr[block, :HEAD].astype(BF16)
        fresh_v = f_scr[block, HEAD : 2 * HEAD].astype(BF16)
        new = lax.dot_general(q, fresh_k, contract, preferred_element_type=F32)
        rel = col_new - 32 * (g % 4)
        new = jnp.where((rel >= 0) & (rel <= row % 4), new, -1e30)
        lengths = [lens_ref[LENGTH, 8 * g + e] for e in range(8)]
        index = [meta_ref[SOURCE + b, 8 * g + e] for e in range(8) for b in range(8)]
        old_a, old_b = [], []
        for k in range(GROUP):
            keys = jnp.concatenate([page_scr[odd, j] for j in index[16 * k : 16 * k + 16]], axis=0)
            old = lax.dot_general(
                q[32 * k : 32 * k + 32], keys, contract, preferred_element_type=F32
            )
            old_a.append(jnp.where(col_a < lengths[2 * k], old[:, :HEAD], -1e30))
            old_b.append(jnp.where(col_b < lengths[2 * k + 1], old[:, HEAD:], -1e30))
        old_a, old_b = jnp.concatenate(old_a, axis=0), jnp.concatenate(old_b, axis=0)
        top = jnp.max(jnp.maximum(jnp.maximum(old_a, old_b), new), axis=1, keepdims=True)
        old_a, old_b, new = (jnp.exp((v - top) * scale) for v in (old_a, old_b, new))
        part = 1.0 / jnp.sum(old_a + old_b + new, axis=1, keepdims=True)
        old = jnp.concatenate([old_a * part, old_b * part], axis=1).astype(BF16)
        mixed = jnp.dot((new * part).astype(BF16), fresh_v, preferred_element_type=F32)
        old_mixed = []
        for k in range(GROUP):
            values = jnp.concatenate(
                [page_scr[1 - odd, j] for j in index[16 * k : 16 * k + 16]], axis=0
            )
            old_mixed.append(
                jnp.dot(old[32 * k : 32 * k + 32], values, preferred_element_type=F32)
            )
        mixed = (mixed + jnp.concatenate(old_mixed, axis=0)).astype(BF16)
        return mixed

    def mix(i, _):
        done = [mixed_rows(i * 4 + j) for j in range(4)]
        for j, mixed in enumerate(done):
            for n in range(2 * GROUP):
                slot = meta_ref[SLOT, (i * 4 + j) * 2 * GROUP + n]
                for h in range(4):
                    lo = n // 2 * 32 + h * 8 + n % 2 * 4
                    out_ref[slot, :, h * HEAD : (h + 1) * HEAD] = mixed[lo : lo + 4]
        return 0

    lax.fori_loop(0, 16, edge, 0)
    stores = fetch(((new_ref, new_hbm),), sem)
    settle(copies[16:])
    lax.fori_loop(0, 4, mix, 0)
    settle(stores + fetch(((out_ref, out_hbm),), sem, 1))


def attend(parity, meta, lens, own, far, rx, kv, kv2, cos, sin, pool, pool2, got, got2):
    outs = (sds((128, 4, 512), BF16), sds(pool.shape, BF16))
    return pl.pallas_call(
        attend_kernel,
        out_shape=outs,
        in_specs=[sspec()] * 3 + [hspec()] * 11,
        out_specs=(hspec(), hspec()),
        scratch_shapes=[pltpu.VMEM(a.shape, a.dtype) for a in (own, far, rx, kv, kv2, cos, sin, *outs)]
        + [
            pltpu.VMEM((512, 512), F32),
            pltpu.VMEM((512, 3 * HEAD), F32),
            pltpu.VMEM((2, ZERO_PAGE + 1, 16, HEAD), BF16),
            pltpu.VMEM((17, 16, HEAD), BF16),
            pltpu.SemaphoreType.DMA((25,)),
        ],
        compiler_params=params(),
        name="attend",
    )(parity, meta, lens, own, far, rx, kv, kv2, cos, sin, pool, pool2, got, got2)


def body(
    tokens,
    query_weight_matrix,
    key_value_weight,
    adapter_down_factors,
    adapter_up_query,
    adapter_up_key_value,
    storage_slot_adapter,
    slot_request_adapter,
    migration,
    lengths,
    previous_block_table,
    moved_block_table,
    paged_cache_pool,
):
    r = lax.axis_index("rep").astype(I32)
    t = lax.axis_index("tp").astype(I32)
    core = t % 2

    def other_core(a):
        return lax.ppermute(a, "tp", [(i, i ^ 1) for i in range(16)])

    def other_x(a):
        return lax.ppermute(a, "tp", [(i, i ^ 2) for i in range(16)])

    def along_y(a, d):
        return lax.ppermute(a, "tp", [(i, (i + 4 * d) % 16) for i in range(16)])

    def swap_rep(a):
        return lax.all_to_all(a, "rep", split_axis=0, concat_axis=0, tiled=True)

    send, own, cand, meta = plan(
        r.reshape(1), migration.reshape(8, 128), slot_request_adapter.reshape(8, 128),
        storage_slot_adapter.reshape(1, 64), lengths.reshape(1, 128),
        previous_block_table.T, moved_block_table.T, tokens.reshape(512, 512),
    )
    packed, leaving = pack(
        meta, adapter_down_factors, adapter_up_query, adapter_up_key_value, paged_cache_pool
    )
    pool2 = other_core(paged_cache_pool)
    vq, vk = other_core(query_weight_matrix), other_core(key_value_weight)
    x, length, lens = join(own, swap_rep(send), meta, packed, pool2)
    far_down = swap_rep(packed)

    weights = (query_weight_matrix, key_value_weight, vq, vk)
    one = core.reshape(1)
    xh = other_x(x)
    yp = along_y(x, 1)
    ym = along_y(x, -1)
    full = (0, 512)
    ends = ((0, (0, 256), 0, 0), (1, (256, 512), 1, 0))
    yp2, ym2 = slices(ends, (256, 256), (yp, ym), (vq, vk))
    y2 = (along_y(yp2, 1), along_y(ym2, -1))

    keep, give = down_product(one, x, adapter_down_factors, far_down, cand)
    total = keep + other_core(give)
    total = total + other_x(total)
    leaving, total, xh, y2 = lax.optimization_barrier((leaving, total, xh, y2))
    got = swap_rep(leaving)

    xyp, xym = along_y(xh, 1), along_y(xh, -1)
    at = t.reshape(1)
    acc = matmul(
        ("far", "own"), at, ((0, 0), (3, 0), (1, 0), (2, 0)),
        (((0, *full),), ((1, *full),), ((2, *full),), ((3, 0, 256), (4, 0, 256))),
        (x, yp, ym, *y2), weights,
    )
    xyp2, xym2 = slices(ends, (256, 256), (xyp, xym), (acc[0],))
    xy2 = (along_y(xyp2, 1), along_y(xym2, -1))
    total = (total + along_y(total, 2)) + (along_y(total, 1) + along_y(total, -1))
    total = total.astype(BF16)
    other_total = other_core(total)
    acc_far, acc_own = matmul(
        ("far", "own"), at, ((0, 1), (3, 1), (1, 1), (2, 1)),
        (((0, *full),), ((1, *full),), ((2, *full),), ((3, 0, 256), (4, 0, 256))),
        (xh, xyp, xym, *xy2), weights, ((acc[0], acc[1]),), (other_total,),
    )
    rx = other_core(acc_far)
    got, acc_own = lax.optimization_barrier((got, acc_own))
    own, kv, cos, sin = up_product(
        one, total, other_total, got, cand, adapter_up_query, adapter_up_key_value, length,
        acc_own,
    )
    return attend(
        one, meta, lens, own, acc_far, rx, kv, other_core(kv), cos, sin,
        paged_cache_pool, pool2, got, other_core(got),
    )


def solution(mesh):
    in_specs = (
        P("rep", None, "tp"),
        P(None, "tp"),
        P(None, "tp"),
        P("rep", "tp", None),
        P("rep", None, "tp"),
        P("rep", None, "tp"),
        P(),
        P(),
        P(),
        P("rep"),
        P("rep", None),
        P("rep", None),
        P("rep", None, "tp"),
    )
    out_specs = (P("rep", None, "tp"), P("rep", None, "tp"))
    return jax.shard_map(body, mesh=mesh, in_specs=in_specs, out_specs=out_specs, check_vma=False)
```

```python
import functools
import math

import jax
import jax.numpy as jnp
import ml_dtypes
import numpy as np
from jax import lax
from jax.experimental import pallas as pl
from jax.experimental.pallas import tpu as pltpu
from jax.sharding import PartitionSpec as P

HEAD = 128
THETA = 500000.0
MIB = 1 << 20
VMEM_MIB = 60
POOL = 1024
ZERO_PAGE = POOL + 512

SLOT, PICK, SOURCE, TARGET, LEAVE = 0, 3, 8, 16, 24
KEPT, LENGTH, FROM = 0, 8, 16

F32 = jnp.float32
BF16 = jnp.bfloat16
I32 = jnp.int32


def iota(shape, axis):
    return lax.broadcasted_iota(I32, shape, axis)


def col_to_row(col):
    n = col.shape[0]
    return jnp.sum(jnp.where(iota((n, n), 0) == iota((n, n), 1), col, 0), axis=0, keepdims=True)


def row_to_col(row, n, stretch=1):
    w = row.shape[1]
    return jnp.sum(
        jnp.where(iota((n, w), 1) == iota((n, w), 0) // stretch, row, 0), axis=1, keepdims=True
    )


def below(mask):
    n = mask.shape[1]
    tri = (iota((n, n), 0) < iota((n, n), 1)).astype(BF16)
    return jnp.dot(mask.astype(BF16), tri, preferred_element_type=F32).astype(I32)


def plan_kernel(
    mig_hbm, sra_hbm, ssa_hbm, len_hbm, prev_hbm, moved_hbm, tok_hbm,
    send_hbm, own_hbm, cand_hbm, meta_hbm,
    mig_ref, sra_ref, ssa_ref, len_ref, prev_ref, moved_ref, tok_ref, send_ref, own_ref, cand_ref, meta_ref, sem,
):
    loads = fetch(
        (
            (mig_hbm, mig_ref), (sra_hbm, sra_ref), (ssa_hbm, ssa_ref), (len_hbm, len_ref),
            (prev_hbm, prev_ref), (moved_hbm, moved_ref), (tok_hbm, tok_ref),
        ),
        sem,
    )
    settle(loads[:6])
    r = lax.axis_index("rep").astype(I32)
    groups, per = mig_ref.shape
    half = per // 2
    mig = mig_ref[...]
    grp, loc = mig // per, mig % per
    drow = iota((groups, per), 0)
    out_mask = ((grp == r) & (drow != r)).astype(I32)
    mine = jnp.sum(jnp.where(drow == r, mig, 0), axis=0, keepdims=True)
    g_in, loc_in = mine // per, mine % per
    in_mask = (g_in == drow).astype(I32)
    ranks = below(jnp.concatenate([out_mask, in_mask], axis=0))
    out_rank, in_ranks = ranks[:groups], ranks[groups:]
    in_rank = jnp.sum(in_mask * in_ranks, axis=0, keepdims=True)
    stay = g_in == r

    parts = []
    for d in range(groups):
        hit = (out_mask[d : d + 1] == 1) & (out_rank[d : d + 1] == iota((groups, per), 0))
        parts.append(jnp.sum(jnp.where(hit, loc[d : d + 1] + 1, 0), axis=1, keepdims=True))
    src_col = jnp.concatenate(parts, axis=0) - 1
    src_row = col_to_row(src_col)

    count = jnp.sum(jnp.where(drow == r, 0, in_mask), axis=1, keepdims=True)
    lane_u = iota((groups, half), 1)
    count_u = jnp.sum(jnp.where(iota((groups, half), 0) == lane_u // groups, count, 0), axis=0, keepdims=True)
    free = (lane_u[:1] % groups >= count_u).astype(I32)
    free_rank = jnp.where(free == 1, below(free), -1)
    free_col = row_to_col(free_rank, half)
    extra = jnp.sum(
        jnp.where(free_col == in_rank - half, iota((half, per), 0), 0), axis=0, keepdims=True
    )
    place = jnp.where(
        stay, jnp.where(in_rank < half, in_rank, half + extra), half + groups * g_in + in_rank
    )
    sel = place == iota((per, per), 0)

    def placed(row):
        return jnp.sum(jnp.where(sel, row, 0), axis=1, keepdims=True)

    slot_row = col_to_row(placed(iota((1, per), 1)))
    loc_row = col_to_row(placed(jnp.where(stay, loc_in, -1)))

    drow_sra = iota(sra_ref.shape, 0)
    sra = sra_ref[...]
    wanted = jnp.sum(jnp.where(drow_sra == r, sra, 0), axis=0, keepdims=True)
    ssa_col = row_to_col(ssa_ref[...], half)
    store = jnp.sum(jnp.where(ssa_col == wanted, iota((half, per), 0), 0), axis=0, keepdims=True)
    cand = jnp.where(store // groups == r, store % groups, groups + store // groups)
    cand_row = col_to_row(placed(cand))
    rows = per * 4
    cand_ref[...] = jnp.broadcast_to(row_to_col(cand_row, rows, 4), (rows, HEAD)).astype(BF16)
    picks = jnp.zeros((groups, 1), I32)
    lane_s = iota((1, half), 1)
    for i in range(groups):
        name = jnp.sum(jnp.where(lane_s == r * groups + i, ssa_ref[...], 0), axis=1, keepdims=True)
        used = jnp.max((sra == name).astype(I32), axis=1, keepdims=True)
        picks = jnp.maximum(picks, used * i)
    pick_row = jnp.sum(
        jnp.where(iota((groups, per), 0) == iota((groups, per), 1), picks, 0), axis=0, keepdims=True
    )

    len_col = jnp.broadcast_to(row_to_col(len_ref[...], rows, 4), (rows, HEAD))
    settle(loads[6:])
    tok = jnp.concatenate([tok_ref[...], len_col.astype(F32).astype(BF16)], axis=1)

    def rows_of(row, n):
        base = row_to_col(row, n, 4)
        at = 4 * base + iota((n, 1), 0) % 4
        pick = (jnp.broadcast_to(at, (n, rows)) == iota((n, rows), 1)) & (base >= 0)
        return jnp.dot(
            jnp.where(pick, 1.0, 0.0).astype(BF16), tok, preferred_element_type=F32
        ).astype(BF16)

    send_ref[...] = rows_of(src_row, rows // 2)
    stores = fetch(((send_ref, send_hbm),), sem)
    own_ref[...] = rows_of(loc_row, rows)
    stores += fetch(((own_ref, own_hbm),), sem, 1)
    src_wide = jnp.sum(
        jnp.where(iota((half, per), 0) == iota((half, per), 1), src_col, 0), axis=0, keepdims=True
    )
    def looked_up(table, row):
        pick = jnp.where(row == iota((per, per), 0), 1.0, 0.0).astype(BF16)
        parts = jnp.concatenate([table // 32, table % 32], axis=0).astype(F32).astype(BF16)
        found = jnp.dot(parts, pick, preferred_element_type=F32).astype(I32)
        return found[:8] * 32 + found[8:]

    prev, moved = prev_ref[...], moved_ref[...]
    lane8, row8 = iota((8, per), 1), iota((8, per), 0)
    source = jnp.where(loc_row >= 0, looked_up(prev, loc_row), POOL + (lane8 - half) * 8 + row8)
    target = looked_up(moved, slot_row)
    leave = looked_up(prev, src_wide)
    zero = jnp.zeros((groups - 4, per), I32)
    meta_ref[...] = jnp.concatenate(
        [slot_row, loc_row, src_wide, pick_row, zero, source, target, leave], axis=0
    )
    stores += fetch(((cand_ref, cand_hbm), (meta_ref, meta_hbm)), sem, 2)
    settle(stores)


def hspec():
    return pl.BlockSpec(memory_space=pltpu.HBM)


def fetch(pairs, sem, at=0):
    copies = [pltpu.make_async_copy(a, b, sem.at[at + n]) for n, (a, b) in enumerate(pairs)]
    for c in copies:
        c.start()
    return copies


def settle(copies):
    for c in copies:
        c.wait()


def sspec():
    return pl.BlockSpec(memory_space=pltpu.SMEM)


def params():
    return pltpu.CompilerParams(vmem_limit_bytes=VMEM_MIB * MIB)


def sds(shape, dtype):
    return jax.ShapeDtypeStruct(shape, dtype)


def plan(mig, sra, ssa, lengths, prev, moved, tok):
    rows = tok.shape[0]
    ins = (mig, sra, ssa, lengths, prev, moved, tok)
    outs = (
        sds((rows // 2, 640), BF16),
        sds((rows, 640), BF16),
        sds((rows, HEAD), BF16),
        sds((32, HEAD), I32),
    )
    return pl.pallas_call(
        plan_kernel,
        out_shape=outs,
        in_specs=[hspec()] * 7,
        out_specs=(hspec(),) * 4,
        scratch_shapes=[pltpu.VMEM(a.shape, a.dtype) for a in ins + outs]
        + [pltpu.SemaphoreType.DMA((7,))],
        compiler_params=params(),
        name="plan",
    )(*ins)


def pack_kernel(
    meta_ref, down_hbm, q_hbm, k_hbm, pool_hbm, down_out, rest_out,
    down_ref, q_ref, k_ref, pool_ref, rest_ref, sem, pool_sem,
):
    pairs = [(down_hbm.at[meta_ref[PICK, d]], down_ref.at[d]) for d in range(8)]
    loads = fetch(pairs, sem)
    later = fetch(((pool_hbm, pool_ref), (q_hbm, q_ref), (k_hbm, k_ref)), pool_sem)
    settle(loads)
    stores = fetch(((down_ref, down_out),), sem)
    settle(later)
    for d in range(8):
        i = meta_ref[PICK, d]
        q = q_ref[i]
        for h in range(4):
            rest_ref[d, 64 + 4 * h : 68 + 4 * h] = q[:, h * HEAD : (h + 1) * HEAD].reshape(4, 16, HEAD)
        rest_ref[d, 80:84] = k_ref[i].reshape(4, 16, HEAD)

    def some(g, _):
        pages = [pool_ref[meta_ref[LEAVE + b, 4 * g + e]] for e in range(4) for b in range(8)]
        for n, page in enumerate(pages):
            rest_ref[g // 2, (g % 2) * 32 + n] = page
        return 0

    lax.fori_loop(0, 16, some, 0)
    settle(stores + fetch(((rest_ref, rest_out),), pool_sem))


def pack(meta, down, up_q, up_kv, pool):
    rest = sds((8, 84, 16, HEAD), BF16)
    return pl.pallas_call(
        pack_kernel,
        out_shape=(sds(down.shape, BF16), rest),
        in_specs=[sspec()] + [hspec()] * 4,
        out_specs=(hspec(), hspec()),
        scratch_shapes=[pltpu.VMEM(a.shape, BF16) for a in (down, up_q, up_kv, pool, rest)]
        + [pltpu.SemaphoreType.DMA((8,)), pltpu.SemaphoreType.DMA((3,))],
        compiler_params=params(),
        name="pack",
    )(meta, down, up_q, up_kv, pool)


def join_kernel(
    own_hbm, got_hbm, meta_hbm, after_ref, after2_ref, x_hbm, len_hbm, lens_hbm,
    own_ref, got_ref, meta_ref, x_ref, len_ref, lens_ref, sem,
):
    settle(fetch(((own_hbm, own_ref), (got_hbm, got_ref), (meta_hbm, meta_ref)), sem))
    rows = x_ref.shape[0]
    x_ref[: rows // 2] = own_ref[: rows // 2, :512]
    x_ref[rows // 2 :] = own_ref[rows // 2 :, :512] + got_ref[:, :512]
    store = fetch(((x_ref, x_hbm),), sem)
    length = jnp.concatenate(
        [own_ref[: rows // 2, 512:], own_ref[rows // 2 :, 512:] + got_ref[:, 512:]], axis=0
    ).astype(F32)
    len_ref[...] = length
    row = jnp.sum(
        jnp.where(iota((rows, HEAD), 0) == 4 * iota((rows, HEAD), 1), length, 0.0),
        axis=0,
        keepdims=True,
    ).astype(I32)
    kept = jnp.clip(row - 16 * iota((8, HEAD), 0), 0, 16)
    lens_ref[KEPT : KEPT + 8] = kept
    lens_ref[LENGTH : LENGTH + 8] = jnp.broadcast_to(row, (8, HEAD))
    lens_ref[FROM : FROM + 8] = jnp.where(kept > 0, meta_ref[SOURCE : SOURCE + 8], ZERO_PAGE)
    settle(store + fetch(((len_ref, len_hbm), (lens_ref, lens_hbm)), sem, 1))


def join(own, got, meta, *after):
    rows = own.shape[0]
    return pl.pallas_call(
        join_kernel,
        out_shape=(sds((rows, 512), BF16), sds((rows, HEAD), F32), sds((24, HEAD), I32)),
        in_specs=[hspec()] * 5,
        out_specs=(hspec(),) * 3,
        scratch_shapes=[
            pltpu.VMEM(own.shape, BF16),
            pltpu.VMEM(got.shape, BF16),
            pltpu.VMEM(meta.shape, I32),
            pltpu.VMEM((rows, 512), BF16),
            pltpu.VMEM((rows, HEAD), F32),
            pltpu.VMEM((24, HEAD), I32),
            pltpu.SemaphoreType.DMA((3,)),
        ],
        compiler_params=params(),
        name="join",
    )(own, got, meta, *after)


def slices_kernel(moves, n, *refs):
    outs = len({m[2] for m in moves})
    ins, dst = refs[:n], refs[-1 - 2 * outs : -1 - outs]
    tmp, sem = refs[-1 - outs : -1], refs[-1]
    loads = fetch(
        [(ins[i].at[lo:hi], tmp[o].at[at : at + hi - lo]) for i, (lo, hi), o, at in moves], sem
    )
    settle(loads)
    settle(fetch([(t, d) for t, d in zip(tmp, dst)], sem))


def slices(moves, rows, arrays, after):
    shapes = [(n, 512) for n in rows]
    return pl.pallas_call(
        functools.partial(slices_kernel, moves, len(arrays)),
        out_shape=tuple(sds(s, BF16) for s in shapes),
        in_specs=[hspec()] * (len(arrays) + len(after)),
        out_specs=(hspec(),) * len(rows),
        scratch_shapes=[pltpu.VMEM(s, BF16) for s in shapes]
        + [pltpu.SemaphoreType.DMA((len(moves),))],
        compiler_params=params(),
        name="slices",
    )(*arrays, *after)


COLUMNS = {"far": ((2, 512, 0), (1, HEAD, 512), (3, HEAD, 640)), "own": ((0, 512, 0),)}
WIDTH = {"far": 768, "own": 512}


def matmul_kernel(blocks, offsets, chunk, n, parts, extra, after, *refs):
    np_, nb = len(parts), len(blocks)
    xs, refs = refs[:n], refs[n:]
    weights, refs = refs[:4], refs[4:]
    adds, refs = refs[: extra * np_], refs[extra * np_ + after :]
    outs, refs = refs[:np_], refs[np_:]
    bufs, refs = refs[:np_], refs[np_:]
    add, refs = refs[: extra * np_], refs[extra * np_ :]
    res, refs = refs[:np_], refs[np_:]
    x_ref, x_sem, sem, add_sem, out_sem = refs
    at = lax.axis_index("tp").astype(I32)
    y, hi, core = at // 4, (at // 2) % 2, at % 2
    place = [(((y + dy) % 4) * 2 + (hi + dx) % 2) * 2 + core for dy, dx in offsets]
    x_loads, w_loads = [], {}
    for k, cut in enumerate(blocks):
        row = 0
        for j, (i, lo, hi) in enumerate(cut):
            to = x_ref.at[row : row + hi - lo, k * 512 : (k + 1) * 512]
            x_loads.append((k, pltpu.make_async_copy(xs[i].at[lo:hi], to, x_sem.at[k, j])))
            row += hi - lo
    for o, part in enumerate(parts):
        for k in range(nb):
            at = pl.ds(pl.multiple_of(place[k] * 512, 512), 512)
            w_loads[o, k] = [
                pltpu.make_async_copy(
                    weights[w].at[at],
                    bufs[o].at[k * 512 : (k + 1) * 512, lo : lo + width],
                    sem.at[k, w],
                )
                for w, width, lo in COLUMNS[part]
            ]
    for k in range(nb):
        for c in [c for at, c in x_loads if at == k] + w_loads[0, k]:
            c.start()
    add_loads = fetch(list(zip(adds, add)), add_sem)
    for o in range(1, np_):
        for k in range(nb):
            for c in w_loads[o, k]:
                c.start()
    stores = []
    for o in range(np_):
        for c in range(0, nb, chunk):
            for k in range(c, c + chunk):
                if o == 0:
                    settle([copy for at, copy in x_loads if at == k])
                settle(w_loads[o, k])
            at = slice(c * 512, (c + chunk) * 512)
            y = jnp.dot(x_ref[:, at], bufs[o][at], preferred_element_type=F32)
            if c == 0:
                settle(add_loads[o * extra : (o + 1) * extra])
                for a in add[o * extra : (o + 1) * extra]:
                    y = y + a[...]
                res[o][...] = y
            else:
                res[o][...] += y
        stores += fetch(((res[o], outs[o]),), out_sem, o)
    settle(stores)


def matmul(parts, offsets, blocks, xs, weights, adds=(), after=(), chunk=4):
    nb = len(blocks)
    outs = tuple(sds((512, WIDTH[p]), F32) for p in parts)
    flat = tuple(a[o] for o in range(len(parts)) for a in adds)
    return pl.pallas_call(
        functools.partial(
            matmul_kernel, blocks, offsets, min(chunk, nb), len(xs), parts, len(adds), len(after)
        ),
        out_shape=outs,
        in_specs=[hspec()] * (len(xs) + 4 + len(flat) + len(after)),
        out_specs=(hspec(),) * len(parts),
        scratch_shapes=[pltpu.VMEM((nb * 512, WIDTH[p]), BF16) for p in parts]
        + [pltpu.VMEM(a.shape, a.dtype) for a in (*flat, *outs)]
        + [
            pltpu.VMEM((512, nb * 512), BF16),
            pltpu.SemaphoreType.DMA((nb, 2)),
            pltpu.SemaphoreType.DMA((nb, 4)),
            pltpu.SemaphoreType.DMA((max(1, len(flat)),)),
            pltpu.SemaphoreType.DMA((len(parts),)),
        ],
        compiler_params=params(),
        name="matmul_" + "_".join(parts),
    )(*xs, *weights, *flat, *after)


def down_kernel(
    x_hbm, here_hbm, far_hbm, cand_hbm, keep_hbm, give_hbm,
    x_ref, here_ref, far_ref, cand_ref, out_ref, sem,
):
    loads = fetch(
        ((x_hbm, x_ref), (here_hbm, here_ref), (cand_hbm, cand_ref), (far_hbm, far_ref)),
        sem,
    )
    settle(loads[:3])
    x = x_ref[...]
    cand = cand_ref[...].astype(F32)
    acc = None
    for a in range(0, 16, 2):
        if a == 8:
            settle(loads[3:])
        ref = here_ref if a < 8 else far_ref
        b = a % 8
        w = jnp.concatenate([ref[b], ref[b + 1]], axis=1)
        y = jnp.dot(x, w, preferred_element_type=F32)
        y = jnp.where(cand == float(a), y[:, :HEAD], jnp.where(cand == float(a + 1), y[:, HEAD:], 0.0))
        acc = y if acc is None else acc + y
    out_ref[...] = acc
    half = out_ref.shape[0] // 2
    core = lax.axis_index("tp").astype(I32) % 2
    mine = pl.ds(pl.multiple_of(core * half, half), half)
    other = pl.ds(pl.multiple_of((1 - core) * half, half), half)
    settle(fetch(((out_ref.at[mine], keep_hbm), (out_ref.at[other], give_hbm)), sem))


def down_product(x, here, far, cand):
    rows = x.shape[0]
    return pl.pallas_call(
        down_kernel,
        out_shape=(sds((rows // 2, HEAD), F32),) * 2,
        in_specs=[hspec()] * 4,
        out_specs=(hspec(), hspec()),
        scratch_shapes=[
            pltpu.VMEM(x.shape, BF16),
            pltpu.VMEM(here.shape, BF16),
            pltpu.VMEM(here.shape, BF16),
            pltpu.VMEM(cand.shape, BF16),
            pltpu.VMEM((rows, HEAD), F32),
            pltpu.SemaphoreType.DMA((4,)),
        ],
        compiler_params=params(),
        name="down_product",
    )(x, here, far, cand)


def turn_table():
    frequency = np.float32(THETA) ** (-(np.arange(HEAD // 2, dtype=np.float32) * 2.0 / HEAD))
    angles = np.arange(HEAD, dtype=np.float32)[:, None] * frequency.astype(np.float32)
    cos, sin = np.cos(angles.astype(np.float64)), np.sin(angles.astype(np.float64))
    rest = np.concatenate([cos, cos, -sin, sin], axis=1).astype(np.float32)
    terms = []
    for _ in range(3):
        terms.append(rest.astype(ml_dtypes.bfloat16))
        rest = rest - terms[-1].astype(np.float32)
    return np.concatenate(terms, axis=1)


def up_kernel(
    mine_hbm, other_hbm, far_hbm, cand_hbm, q_hbm, k_hbm, len_hbm, table_hbm, acc_hbm,
    out_hbm, kv_hbm, cos_hbm, sin_hbm,
    down_ref, far, cand_ref, q_here, k_here, len_ref, table_ref, acc_ref,
    out_ref, kv_ref, cos_ref, sin_ref, sem,
):
    half = mine_hbm.shape[0]
    core = lax.axis_index("tp").astype(I32) % 2
    mine = pl.ds(pl.multiple_of(core * half, half), half)
    other = pl.ds(pl.multiple_of((1 - core) * half, half), half)
    settle(
        fetch(
            (
                (mine_hbm, down_ref.at[mine]), (other_hbm, down_ref.at[other]),
                (far_hbm.at[:, 64:], far), (cand_hbm, cand_ref), (q_hbm, q_here),
                (k_hbm, k_here), (len_hbm, len_ref), (table_hbm, table_ref), (acc_hbm, acc_ref),
            ),
            sem,
        )
    )
    down = down_ref[...].astype(F32)
    cand = cand_ref[...].astype(F32)
    rows = down.shape[0]
    lane = iota((rows, HEAD), 1)
    upper = lane >= HEAD // 2
    other = pltpu.roll(down, HEAD // 2, 1)
    down_q = jnp.where(upper, other, down)
    down_k = jnp.where(upper, down, other)
    shift = jnp.where(upper, 1.0, 0.0)

    def spread(v):
        return jnp.concatenate(
            [jnp.where(cand == shift + float(2 * i), v, 0.0).astype(BF16) for i in range(8)], axis=1
        )

    sq, sk = spread(down_q), spread(down_k)
    q_all, k_all = q_here[...].reshape(512, 512), k_here[...].reshape(512, HEAD)

    def far_part(lo):
        return jnp.concatenate(
            [far[a, lo // 16 : lo // 16 + 4].reshape(64, HEAD) for a in range(8)], axis=0
        )

    w = [
        jnp.concatenate([q_all[:, h * HEAD : (h + 1) * HEAD], far_part(64 * h)], axis=0)
        for h in range(4)
    ]
    for h in (0, 2):
        at = slice(h * HEAD, (h + 2) * HEAD)
        out_ref[:, at] = acc_ref[:, at] + jnp.dot(
            sq, jnp.concatenate([w[h], w[h + 1]], axis=1), preferred_element_type=F32
        )
    kv_ref[...] = jnp.dot(
        sk, jnp.concatenate([k_all, far_part(256)], axis=0), preferred_element_type=F32
    )
    position = len_ref[...].astype(I32) + iota((rows, HEAD), 0) % 4
    pick = jnp.where(position == lane, 1.0, 0.0).astype(BF16)
    turns = jnp.dot(pick, table_ref[...], preferred_element_type=F32)
    turns = turns[:, :256] + turns[:, 256:512] + turns[:, 512:]
    cos_ref[...] = turns[:, :HEAD]
    sin_ref[...] = turns[:, HEAD:]
    settle(
        fetch(
            ((out_ref, out_hbm), (kv_ref, kv_hbm), (cos_ref, cos_hbm), (sin_ref, sin_hbm)), sem
        )
    )


def up_product(mine, other, far, cand, up_q, up_kv, length, acc):
    rows = cand.shape[0]
    ins = (cand, up_q, up_kv, length, jnp.asarray(turn_table()), acc)
    outs = (sds((rows, 512), F32),) + (sds((rows, HEAD), F32),) * 3
    return pl.pallas_call(
        up_kernel,
        out_shape=outs,
        in_specs=[hspec()] * 9,
        out_specs=(hspec(),) * 4,
        scratch_shapes=[pltpu.VMEM((rows, HEAD), BF16), pltpu.VMEM((8, 20, 16, HEAD), BF16)]
        + [pltpu.VMEM(a.shape, a.dtype) for a in ins + outs]
        + [pltpu.SemaphoreType.DMA((9,))],
        compiler_params=params(),
        name="up_product",
    )(mine, other, far, *ins)


GROUP = 4


def page_masks(mask_scr):
    for d in range(17):
        mask_scr[d] = jnp.where(iota((16, HEAD), 0) < d, 1.0, 0.0).astype(BF16)


def attend_kernel(
    meta_hbm, lens_hbm, own_hbm, far_hbm, rx_hbm, kv_hbm, kv2_hbm, cos_hbm, sin_hbm,
    pool_hbm, pool2_hbm, got_hbm, got2_hbm,
    out_hbm, new_hbm,
    meta_ref, lens_ref, own_ref, far_ref, rx_ref, kv_ref, kv2_ref, cos_ref, sin_ref, out_ref, new_ref,
    q_scr, f_scr, page_scr, mask_scr, sem,
):
    odd = lax.axis_index("tp").astype(I32) % 2
    def pages_from(i, pool, got):
        return [(pool, page_scr.at[i, :POOL])] + [
            (got.at[g, :64], page_scr.at[i, POOL + 64 * g : POOL + 64 * g + 64]) for g in range(8)
        ]

    copies = fetch(
        (
            (meta_hbm, meta_ref), (lens_hbm, lens_ref), *pages_from(0, pool_hbm, got_hbm),
            (far_hbm.at[:, 512:], far_ref), (rx_hbm, rx_ref), (kv_hbm, kv_ref), (kv2_hbm, kv2_ref),
            (cos_hbm, cos_ref), (sin_hbm, sin_ref), (own_hbm, own_ref),
            *pages_from(1, pool2_hbm, got2_hbm),
        ),
        sem,
    )
    page_masks(mask_scr)
    page_scr[0, ZERO_PAGE] = jnp.zeros((16, HEAD), BF16)
    settle(copies[:3])

    def keep(g, _):
        kept = []
        for e in range(4):
            for b in range(8):
                p = 4 * g + e
                kept.append((meta_ref[TARGET + b, p], page_scr[0, lens_ref[FROM + b, p]]))
        for at, page in kept:
            new_ref[at] = page
        return 0

    lax.fori_loop(0, 16, keep, 0)
    settle(copies[3:11])
    lax.fori_loop(16, 32, keep, 0)
    settle(copies[11:18])
    cos, sin = cos_ref[...], sin_ref[...]

    def turn(v):
        return v * cos + pltpu.roll(v, HEAD // 2, 1) * sin

    for h in range(4):
        at = slice(h * HEAD, (h + 1) * HEAD)
        q_scr[:, at] = turn(own_ref[:, at] + rx_ref[:, at])
    kv_own = far_ref[:, :HEAD] + rx_ref[:, 640:768] + kv_ref[...]
    kv_oth = far_ref[:, HEAD:] + rx_ref[:, 512:640] + kv2_ref[...]
    key = turn(jnp.where(odd == 0, kv_own, kv_oth))
    value = jnp.where(odd == 0, kv_oth, kv_own)
    f_scr[:, :HEAD] = key
    f_scr[:, HEAD : 2 * HEAD] = value
    f_scr[:, 2 * HEAD :] = jnp.where(odd == 0, key, value)

    gap = jnp.where(
        iota((256, 32), 0) // 32 == iota((256, 32), 1) // 4,
        iota((256, 32), 0) % 32 - iota((256, 32), 1) % 4,
        -1,
    )
    c32 = iota((1, 32), 1) // 4

    def edge_pages(g):
        at = [8 * g + e for e in range(8)]
        lengths = [lens_ref[LENGTH, p] for p in at]
        first = [jnp.minimum(n // 16, 6) for n in lengths]
        fresh = f_scr[pl.ds(pl.multiple_of(32 * g, 32), 32), 2 * HEAD :].astype(BF16)
        start = jnp.zeros((1, 32), I32)
        for e in range(8):
            start = jnp.where(c32 == e, lengths[e] - 16 * first[e], start)
        land = jnp.where(gap == start, 1.0, 0.0).astype(BF16)
        placed = jnp.dot(land, fresh, preferred_element_type=F32).astype(BF16)
        done = []
        for e, p in enumerate(at):
            for k in range(2):
                b = first[e] + k
                lo = e * 32 + k * 16
                page = page_scr[0, meta_ref[SOURCE + b, p]] * mask_scr[lens_ref[KEPT + b, p]]
                done.append((meta_ref[TARGET + b, p], page + placed[lo : lo + 16]))
        return done

    def edge(i, _):
        done = [pair for j in range(2) for pair in edge_pages(2 * i + j)]
        for to, page in done:
            new_ref[to] = page
        return 0

    scale = 1.0 / math.sqrt(HEAD)
    row2 = (iota((32, HEAD), 0) % 8) // 4
    lane32 = iota((32, HEAD), 1)
    col_a = jnp.where(row2 == 0, lane32, HEAD)
    col_b = jnp.where(row2 == 1, lane32, HEAD)
    row = iota((HEAD, HEAD), 0)
    col_new = iota((HEAD, HEAD), 1) - (row // 32) * 8 - (row % 8) // 4 * 4
    contract = (((1,), (1,)), ((), ()))

    def mixed_rows(g):
        q32 = q_scr[pl.ds(pl.multiple_of(32 * g, 32), 32), :]
        q = jnp.concatenate(
            [
                q32[8 * k : 8 * k + 8, h * HEAD : (h + 1) * HEAD]
                for k in range(GROUP)
                for h in range(4)
            ],
            axis=0,
        ).astype(BF16)
        block = pl.ds(pl.multiple_of((g // 4) * HEAD, HEAD), HEAD)
        fresh_k = f_scr[block, :HEAD].astype(BF16)
        fresh_v = f_scr[block, HEAD : 2 * HEAD].astype(BF16)
        new = lax.dot_general(q, fresh_k, contract, preferred_element_type=F32)
        rel = col_new - 32 * (g % 4)
        new = jnp.where((rel >= 0) & (rel <= row % 4), new, -1e30)
        lengths = [lens_ref[LENGTH, 8 * g + e] for e in range(8)]
        index = [meta_ref[SOURCE + b, 8 * g + e] for e in range(8) for b in range(8)]
        old_a, old_b = [], []
        for k in range(GROUP):
            keys = jnp.concatenate([page_scr[odd, j] for j in index[16 * k : 16 * k + 16]], axis=0)
            old = lax.dot_general(
                q[32 * k : 32 * k + 32], keys, contract, preferred_element_type=F32
            )
            old_a.append(jnp.where(col_a < lengths[2 * k], old[:, :HEAD], -1e30))
            old_b.append(jnp.where(col_b < lengths[2 * k + 1], old[:, HEAD:], -1e30))
        old_a, old_b = jnp.concatenate(old_a, axis=0), jnp.concatenate(old_b, axis=0)
        top = jnp.max(jnp.maximum(jnp.maximum(old_a, old_b), new), axis=1, keepdims=True)
        old_a, old_b, new = (jnp.exp((v - top) * scale) for v in (old_a, old_b, new))
        part = 1.0 / jnp.sum(old_a + old_b + new, axis=1, keepdims=True)
        old = jnp.concatenate([old_a * part, old_b * part], axis=1).astype(BF16)
        mixed = jnp.dot((new * part).astype(BF16), fresh_v, preferred_element_type=F32)
        old_mixed = []
        for k in range(GROUP):
            values = jnp.concatenate(
                [page_scr[1 - odd, j] for j in index[16 * k : 16 * k + 16]], axis=0
            )
            old_mixed.append(
                jnp.dot(old[32 * k : 32 * k + 32], values, preferred_element_type=F32)
            )
        mixed = (mixed + jnp.concatenate(old_mixed, axis=0)).astype(BF16)
        return mixed

    def mix(i, _):
        done = [mixed_rows(i * 4 + j) for j in range(4)]
        for j, mixed in enumerate(done):
            for n in range(2 * GROUP):
                slot = meta_ref[SLOT, (i * 4 + j) * 2 * GROUP + n]
                for h in range(4):
                    lo = n // 2 * 32 + h * 8 + n % 2 * 4
                    out_ref[slot, :, h * HEAD : (h + 1) * HEAD] = mixed[lo : lo + 4]
        return 0

    lax.fori_loop(0, 8, edge, 0)
    stores = fetch(((new_ref, new_hbm),), sem)
    settle(copies[18:])
    lax.fori_loop(0, 4, mix, 0)
    settle(stores + fetch(((out_ref, out_hbm),), sem, 1))


def attend(meta, lens, own, far, rx, kv, kv2, cos, sin, pool, pool2, got, got2):
    outs = (sds((128, 4, 512), BF16), sds(pool.shape, BF16))
    return pl.pallas_call(
        attend_kernel,
        out_shape=outs,
        in_specs=[hspec()] * 13,
        out_specs=(hspec(), hspec()),
        scratch_shapes=[pltpu.SMEM(meta.shape, I32), pltpu.SMEM(lens.shape, I32)]
        + [
            pltpu.VMEM(a.shape, a.dtype)
            for a in (own, sds((512, 256), F32), rx, kv, kv2, cos, sin, *outs)
        ]
        + [
            pltpu.VMEM((512, 512), F32),
            pltpu.VMEM((512, 3 * HEAD), F32),
            pltpu.VMEM((2, ZERO_PAGE + 1, 16, HEAD), BF16),
            pltpu.VMEM((17, 16, HEAD), BF16),
            pltpu.SemaphoreType.DMA((27,)),
        ],
        compiler_params=params(),
        name="attend",
    )(meta, lens, own, far, rx, kv, kv2, cos, sin, pool, pool2, got, got2)


def body(
    tokens,
    query_weight_matrix,
    key_value_weight,
    adapter_down_factors,
    adapter_up_query,
    adapter_up_key_value,
    storage_slot_adapter,
    slot_request_adapter,
    migration,
    lengths,
    previous_block_table,
    moved_block_table,
    paged_cache_pool,
):
    def other_core(a):
        return lax.ppermute(a, "tp", [(i, i ^ 1) for i in range(16)])

    def other_x(a):
        return lax.ppermute(a, "tp", [(i, i ^ 2) for i in range(16)])

    def along_y(a, d):
        return lax.ppermute(a, "tp", [(i, (i + 4 * d) % 16) for i in range(16)])

    def swap_rep(a):
        return lax.all_to_all(a, "rep", split_axis=0, concat_axis=0, tiled=True)

    send, own, cand, meta = plan(
        migration.reshape(8, 128), slot_request_adapter.reshape(8, 128),
        storage_slot_adapter.reshape(1, 64), lengths.reshape(1, 128),
        previous_block_table.T, moved_block_table.T, tokens.reshape(512, 512),
    )
    packed, leaving = pack(
        meta, adapter_down_factors, adapter_up_query, adapter_up_key_value, paged_cache_pool
    )
    pool2 = other_core(paged_cache_pool)
    vq, vk = other_core(query_weight_matrix), other_core(key_value_weight)
    x, length, lens = join(own, swap_rep(send), meta, packed, pool2)
    far_down = swap_rep(packed)

    weights = (query_weight_matrix, key_value_weight, vq, vk)
    xh = other_x(x)
    yp = along_y(x, 1)
    ym = along_y(x, -1)
    full = (0, 512)
    ends = ((0, (0, 256), 0, 0), (1, (256, 512), 1, 0))
    yp2, ym2 = slices(ends, (256, 256), (yp, ym), (vq, vk))
    y2 = (along_y(yp2, 1), along_y(ym2, -1))

    keep, give = down_product(x, adapter_down_factors, far_down, cand)
    total = keep + other_core(give)
    total = total + other_x(total)
    leaving, total, _, _ = lax.optimization_barrier((leaving, total, xh, y2))
    got = swap_rep(leaving)

    xyp, xym = along_y(xh, 1), along_y(xh, -1)
    acc = matmul(
        ("far", "own"), ((0, 0), (3, 0), (1, 0), (2, 0)),
        (((0, *full),), ((1, *full),), ((2, *full),), ((3, 0, 256), (4, 0, 256))),
        (x, yp, ym, *y2), weights,
    )
    xyp2, xym2 = slices(ends, (256, 256), (xyp, xym), (acc[0],))
    xy2 = (along_y(xyp2, 1), along_y(xym2, -1))
    total = (total + along_y(total, 2)) + (along_y(total, 1) + along_y(total, -1))
    total = total.astype(BF16)
    other_total = other_core(total)
    acc_far, acc_own = matmul(
        ("far", "own"), ((0, 1), (3, 1), (1, 1), (2, 1)),
        (((0, *full),), ((1, *full),), ((2, *full),), ((3, 0, 256), (4, 0, 256))),
        (xh, xyp, xym, *xy2), weights, ((acc[0], acc[1]),), (other_total,),
    )
    rx = other_core(acc_far)
    got, acc_own = lax.optimization_barrier((got, acc_own))
    own, kv, cos, sin = up_product(
        total, other_total, got, cand, adapter_up_query, adapter_up_key_value, length, acc_own
    )
    return attend(
        meta, lens, own, acc_far, rx, kv, other_core(kv), cos, sin,
        paged_cache_pool, pool2, got, other_core(got),
    )


def solution(mesh):
    in_specs = (
        P("rep", None, "tp"),
        P(None, "tp"),
        P(None, "tp"),
        P("rep", "tp", None),
        P("rep", None, "tp"),
        P("rep", None, "tp"),
        P(),
        P(),
        P(),
        P("rep"),
        P("rep", None),
        P("rep", None),
        P("rep", None, "tp"),
    )
    out_specs = (P("rep", None, "tp"), P("rep", None, "tp"))
    return jax.shard_map(body, mesh=mesh, in_specs=in_specs, out_specs=out_specs, check_vma=False)
```

```python
import functools
import math

import jax
import jax.numpy as jnp
import ml_dtypes
import numpy as np
from jax import lax
from jax.experimental import pallas as pl
from jax.experimental.pallas import tpu as pltpu
from jax.sharding import PartitionSpec as P

HEAD = 128
THETA = 500000.0
MIB = 1 << 20
VMEM_MIB = 60
POOL = 1024
ZERO_PAGE = POOL + 512

SLOT, PICK, SOURCE, TARGET, LEAVE = 0, 3, 8, 16, 24
KEPT, LENGTH, FROM = 0, 8, 16

F32 = jnp.float32
BF16 = jnp.bfloat16
I32 = jnp.int32


def iota(shape, axis):
    return lax.broadcasted_iota(I32, shape, axis)


def col_to_row(col):
    n = col.shape[0]
    return jnp.sum(jnp.where(iota((n, n), 0) == iota((n, n), 1), col, 0), axis=0, keepdims=True)


def row_to_col(row, n, stretch=1):
    w = row.shape[1]
    return jnp.sum(
        jnp.where(iota((n, w), 1) == iota((n, w), 0) // stretch, row, 0), axis=1, keepdims=True
    )


def below(mask):
    n = mask.shape[1]
    tri = (iota((n, n), 0) < iota((n, n), 1)).astype(BF16)
    return jnp.dot(mask.astype(BF16), tri, preferred_element_type=F32).astype(I32)


def plan_kernel(
    mig_hbm, sra_hbm, ssa_hbm, len_hbm, prev_hbm, moved_hbm, tok_hbm,
    send_hbm, own_hbm, cand_hbm, meta_hbm,
    mig_ref, sra_ref, ssa_ref, len_ref, prev_ref, moved_ref, tok_ref, send_ref, own_ref, cand_ref, meta_ref, sem,
):
    loads = fetch(
        (
            (mig_hbm, mig_ref), (sra_hbm, sra_ref), (ssa_hbm, ssa_ref), (len_hbm, len_ref),
            (prev_hbm, prev_ref), (moved_hbm, moved_ref), (tok_hbm, tok_ref),
        ),
        sem,
    )
    settle(loads[:6])
    r = lax.axis_index("rep").astype(I32)
    groups, per = mig_ref.shape
    half = per // 2
    mig = mig_ref[...]
    grp, loc = mig // per, mig % per
    drow = iota((groups, per), 0)
    out_mask = ((grp == r) & (drow != r)).astype(I32)
    mine = jnp.sum(jnp.where(drow == r, mig, 0), axis=0, keepdims=True)
    g_in, loc_in = mine // per, mine % per
    in_mask = (g_in == drow).astype(I32)
    ranks = below(jnp.concatenate([out_mask, in_mask], axis=0))
    out_rank, in_ranks = ranks[:groups], ranks[groups:]
    in_rank = jnp.sum(in_mask * in_ranks, axis=0, keepdims=True)
    stay = g_in == r

    parts = []
    for d in range(groups):
        hit = (out_mask[d : d + 1] == 1) & (out_rank[d : d + 1] == iota((groups, per), 0))
        parts.append(jnp.sum(jnp.where(hit, loc[d : d + 1] + 1, 0), axis=1, keepdims=True))
    src_col = jnp.concatenate(parts, axis=0) - 1
    src_row = col_to_row(src_col)

    count = jnp.sum(jnp.where(drow == r, 0, in_mask), axis=1, keepdims=True)
    lane_u = iota((groups, half), 1)
    count_u = jnp.sum(jnp.where(iota((groups, half), 0) == lane_u // groups, count, 0), axis=0, keepdims=True)
    free = (lane_u[:1] % groups >= count_u).astype(I32)
    free_rank = jnp.where(free == 1, below(free), -1)
    free_col = row_to_col(free_rank, half)
    extra = jnp.sum(
        jnp.where(free_col == in_rank - half, iota((half, per), 0), 0), axis=0, keepdims=True
    )
    place = jnp.where(
        stay, jnp.where(in_rank < half, in_rank, half + extra), half + groups * g_in + in_rank
    )
    sel = place == iota((per, per), 0)

    def placed(row):
        return jnp.sum(jnp.where(sel, row, 0), axis=1, keepdims=True)

    slot_row = col_to_row(placed(iota((1, per), 1)))
    loc_row = col_to_row(placed(jnp.where(stay, loc_in, -1)))

    drow_sra = iota(sra_ref.shape, 0)
    sra = sra_ref[...]
    wanted = jnp.sum(jnp.where(drow_sra == r, sra, 0), axis=0, keepdims=True)
    ssa_col = row_to_col(ssa_ref[...], half)
    store = jnp.sum(jnp.where(ssa_col == wanted, iota((half, per), 0), 0), axis=0, keepdims=True)
    cand = jnp.where(store // groups == r, store % groups, groups + store // groups)
    cand_row = col_to_row(placed(cand))
    rows = per * 4
    cand_ref[...] = jnp.broadcast_to(row_to_col(cand_row, rows, 4), (rows, HEAD)).astype(BF16)
    picks = jnp.zeros((groups, 1), I32)
    lane_s = iota((1, half), 1)
    for i in range(groups):
        name = jnp.sum(jnp.where(lane_s == r * groups + i, ssa_ref[...], 0), axis=1, keepdims=True)
        used = jnp.max((sra == name).astype(I32), axis=1, keepdims=True)
        picks = jnp.maximum(picks, used * i)
    pick_row = jnp.sum(
        jnp.where(iota((groups, per), 0) == iota((groups, per), 1), picks, 0), axis=0, keepdims=True
    )

    len_col = jnp.broadcast_to(row_to_col(len_ref[...], rows, 4), (rows, HEAD))
    settle(loads[6:])
    tok3 = tok_ref[...]
    tok = jnp.concatenate([tok3.reshape(rows, tok3.shape[2]), len_col.astype(F32).astype(BF16)], axis=1)

    def rows_of(row, n):
        base = row_to_col(row, n, 4)
        at = 4 * base + iota((n, 1), 0) % 4
        pick = (jnp.broadcast_to(at, (n, rows)) == iota((n, rows), 1)) & (base >= 0)
        return jnp.dot(
            jnp.where(pick, 1.0, 0.0).astype(BF16), tok, preferred_element_type=F32
        ).astype(BF16)

    send_ref[...] = rows_of(src_row, rows // 2)
    stores = fetch(((send_ref, send_hbm),), sem)
    own_ref[...] = rows_of(loc_row, rows)
    stores += fetch(((own_ref, own_hbm),), sem, 1)
    src_wide = jnp.sum(
        jnp.where(iota((half, per), 0) == iota((half, per), 1), src_col, 0), axis=0, keepdims=True
    )
    def looked_up(table, row):
        pick = jnp.where(row == iota((per, per), 0), 1.0, 0.0).astype(BF16)
        parts = jnp.concatenate([table // 32, table % 32], axis=0).astype(F32).astype(BF16)
        found = jnp.dot(parts, pick, preferred_element_type=F32).astype(I32)
        return found[:8] * 32 + found[8:]

    prev, moved = prev_ref[...], moved_ref[...]
    lane8, row8 = iota((8, per), 1), iota((8, per), 0)
    source = jnp.where(loc_row >= 0, looked_up(prev, loc_row), POOL + (lane8 - half) * 8 + row8)
    target = looked_up(moved, slot_row)
    leave = looked_up(prev, src_wide)
    zero = jnp.zeros((groups - 4, per), I32)
    meta_ref[...] = jnp.concatenate(
        [slot_row, loc_row, src_wide, pick_row, zero, source, target, leave], axis=0
    )
    stores += fetch(((cand_ref, cand_hbm), (meta_ref, meta_hbm)), sem, 2)
    settle(stores)


def hspec():
    return pl.BlockSpec(memory_space=pltpu.HBM)


def fetch(pairs, sem, at=0):
    copies = [pltpu.make_async_copy(a, b, sem.at[at + n]) for n, (a, b) in enumerate(pairs)]
    for c in copies:
        c.start()
    return copies


def settle(copies):
    for c in copies:
        c.wait()


def sspec():
    return pl.BlockSpec(memory_space=pltpu.SMEM)


def params():
    return pltpu.CompilerParams(vmem_limit_bytes=VMEM_MIB * MIB)


def sds(shape, dtype):
    return jax.ShapeDtypeStruct(shape, dtype)


def plan(mig, sra, ssa, lengths, prev, moved, tok):
    rows = tok.shape[0] * tok.shape[1]
    ins = (mig, sra, ssa, lengths, prev, moved, tok)
    outs = (
        sds((rows // 2, 640), BF16),
        sds((rows, 640), BF16),
        sds((rows, HEAD), BF16),
        sds((32, HEAD), I32),
    )
    return pl.pallas_call(
        plan_kernel,
        out_shape=outs,
        in_specs=[hspec()] * 7,
        out_specs=(hspec(),) * 4,
        scratch_shapes=[pltpu.VMEM(a.shape, a.dtype) for a in ins + outs]
        + [pltpu.SemaphoreType.DMA((7,))],
        compiler_params=params(),
        name="plan",
    )(*ins)


def pack_kernel(
    meta_ref, down_hbm, q_hbm, k_hbm, pool_hbm, down_out, rest_out,
    down_ref, q_ref, k_ref, pool_ref, rest_ref, sem, pool_sem,
):
    pairs = [(down_hbm.at[meta_ref[PICK, d]], down_ref.at[d]) for d in range(8)]
    loads = fetch(pairs, sem)
    later = fetch(((pool_hbm, pool_ref), (q_hbm, q_ref), (k_hbm, k_ref)), pool_sem)
    settle(loads)
    stores = fetch(((down_ref, down_out),), sem)
    settle(later)
    for d in range(8):
        i = meta_ref[PICK, d]
        q = q_ref[i]
        for h in range(4):
            rest_ref[d, 64 + 4 * h : 68 + 4 * h] = q[:, h * HEAD : (h + 1) * HEAD].reshape(4, 16, HEAD)
        rest_ref[d, 80:84] = k_ref[i].reshape(4, 16, HEAD)

    def some(g, _):
        pages = [pool_ref[meta_ref[LEAVE + b, 4 * g + e]] for e in range(4) for b in range(8)]
        for n, page in enumerate(pages):
            rest_ref[g // 2, (g % 2) * 32 + n] = page
        return 0

    lax.fori_loop(0, 16, some, 0)
    settle(stores + fetch(((rest_ref, rest_out),), pool_sem))


def pack(meta, down, up_q, up_kv, pool):
    rest = sds((8, 84, 16, HEAD), BF16)
    return pl.pallas_call(
        pack_kernel,
        out_shape=(sds(down.shape, BF16), rest),
        in_specs=[sspec()] + [hspec()] * 4,
        out_specs=(hspec(), hspec()),
        scratch_shapes=[pltpu.VMEM(a.shape, BF16) for a in (down, up_q, up_kv, pool, rest)]
        + [pltpu.SemaphoreType.DMA((8,)), pltpu.SemaphoreType.DMA((3,))],
        compiler_params=params(),
        name="pack",
    )(meta, down, up_q, up_kv, pool)


def join_kernel(
    own_hbm, got_hbm, meta_hbm, after_ref, after2_ref, x_hbm, len_hbm, lens_hbm,
    own_ref, got_ref, meta_ref, x_ref, len_ref, lens_ref, sem,
):
    settle(fetch(((own_hbm, own_ref), (got_hbm, got_ref), (meta_hbm, meta_ref)), sem))
    rows = x_ref.shape[0]
    x_ref[: rows // 2] = own_ref[: rows // 2, :512]
    x_ref[rows // 2 :] = own_ref[rows // 2 :, :512] + got_ref[:, :512]
    store = fetch(((x_ref, x_hbm),), sem)
    length = jnp.concatenate(
        [own_ref[: rows // 2, 512:], own_ref[rows // 2 :, 512:] + got_ref[:, 512:]], axis=0
    ).astype(F32)
    len_ref[...] = length
    row = jnp.sum(
        jnp.where(iota((rows, HEAD), 0) == 4 * iota((rows, HEAD), 1), length, 0.0),
        axis=0,
        keepdims=True,
    ).astype(I32)
    kept = jnp.clip(row - 16 * iota((8, HEAD), 0), 0, 16)
    lens_ref[KEPT : KEPT + 8] = kept
    lens_ref[LENGTH : LENGTH + 8] = jnp.broadcast_to(row, (8, HEAD))
    lens_ref[FROM : FROM + 8] = jnp.where(kept > 0, meta_ref[SOURCE : SOURCE + 8], ZERO_PAGE)
    settle(store + fetch(((len_ref, len_hbm), (lens_ref, lens_hbm)), sem, 1))


def join(own, got, meta, *after):
    rows = own.shape[0]
    return pl.pallas_call(
        join_kernel,
        out_shape=(sds((rows, 512), BF16), sds((rows, HEAD), F32), sds((24, HEAD), I32)),
        in_specs=[hspec()] * 5,
        out_specs=(hspec(),) * 3,
        scratch_shapes=[
            pltpu.VMEM(own.shape, BF16),
            pltpu.VMEM(got.shape, BF16),
            pltpu.VMEM(meta.shape, I32),
            pltpu.VMEM((rows, 512), BF16),
            pltpu.VMEM((rows, HEAD), F32),
            pltpu.VMEM((24, HEAD), I32),
            pltpu.SemaphoreType.DMA((3,)),
        ],
        compiler_params=params(),
        name="join",
    )(own, got, meta, *after)


def slices_kernel(moves, n, *refs):
    outs = len({m[2] for m in moves})
    ins, dst = refs[:n], refs[-1 - 2 * outs : -1 - outs]
    tmp, sem = refs[-1 - outs : -1], refs[-1]
    loads = fetch(
        [(ins[i].at[lo:hi], tmp[o].at[at : at + hi - lo]) for i, (lo, hi), o, at in moves], sem
    )
    settle(loads)
    settle(fetch([(t, d) for t, d in zip(tmp, dst)], sem))


def slices(moves, rows, arrays, after):
    shapes = [(n, 512) for n in rows]
    return pl.pallas_call(
        functools.partial(slices_kernel, moves, len(arrays)),
        out_shape=tuple(sds(s, BF16) for s in shapes),
        in_specs=[hspec()] * (len(arrays) + len(after)),
        out_specs=(hspec(),) * len(rows),
        scratch_shapes=[pltpu.VMEM(s, BF16) for s in shapes]
        + [pltpu.SemaphoreType.DMA((len(moves),))],
        compiler_params=params(),
        name="slices",
    )(*arrays, *after)


COLUMNS = {"far": ((2, 512, 0), (1, HEAD, 512), (3, HEAD, 640)), "own": ((0, 512, 0),)}
WIDTH = {"far": 768, "own": 512}


def matmul_kernel(blocks, offsets, chunk, n, parts, extra, after, *refs):
    np_, nb = len(parts), len(blocks)
    xs, refs = refs[:n], refs[n:]
    weights, refs = refs[:4], refs[4:]
    adds, refs = refs[: extra * np_], refs[extra * np_ + after :]
    outs, refs = refs[:np_], refs[np_:]
    bufs, refs = refs[:np_], refs[np_:]
    add, refs = refs[: extra * np_], refs[extra * np_ :]
    res, refs = refs[:np_], refs[np_:]
    x_ref, x_sem, sem, add_sem, out_sem = refs
    at = lax.axis_index("tp").astype(I32)
    y, hi, core = at // 4, (at // 2) % 2, at % 2
    place = [(((y + dy) % 4) * 2 + (hi + dx) % 2) * 2 + core for dy, dx in offsets]
    x_loads, w_loads = [], {}
    for k, cut in enumerate(blocks):
        row = 0
        for j, (i, lo, hi) in enumerate(cut):
            to = x_ref.at[row : row + hi - lo, k * 512 : (k + 1) * 512]
            x_loads.append((k, pltpu.make_async_copy(xs[i].at[lo:hi], to, x_sem.at[k, j])))
            row += hi - lo
    for o, part in enumerate(parts):
        for k in range(nb):
            at = pl.ds(pl.multiple_of(place[k] * 512, 512), 512)
            w_loads[o, k] = [
                pltpu.make_async_copy(
                    weights[w].at[at],
                    bufs[o].at[k * 512 : (k + 1) * 512, lo : lo + width],
                    sem.at[k, w],
                )
                for w, width, lo in COLUMNS[part]
            ]
    for k in range(nb):
        for c in [c for at, c in x_loads if at == k] + w_loads[0, k]:
            c.start()
    add_loads = fetch(list(zip(adds, add)), add_sem)
    for o in range(1, np_):
        for k in range(nb):
            for c in w_loads[o, k]:
                c.start()
    stores = []
    for o in range(np_):
        for c in range(0, nb, chunk):
            for k in range(c, c + chunk):
                if o == 0:
                    settle([copy for at, copy in x_loads if at == k])
                settle(w_loads[o, k])
            at = slice(c * 512, (c + chunk) * 512)
            y = jnp.dot(x_ref[:, at], bufs[o][at], preferred_element_type=F32)
            if c == 0:
                settle(add_loads[o * extra : (o + 1) * extra])
                for a in add[o * extra : (o + 1) * extra]:
                    y = y + a[...]
                res[o][...] = y
            else:
                res[o][...] += y
        stores += fetch(((res[o], outs[o]),), out_sem, o)
    settle(stores)


def matmul(parts, offsets, blocks, xs, weights, adds=(), after=(), chunk=4):
    nb = len(blocks)
    outs = tuple(sds((512, WIDTH[p]), F32) for p in parts)
    flat = tuple(a[o] for o in range(len(parts)) for a in adds)
    return pl.pallas_call(
        functools.partial(
            matmul_kernel, blocks, offsets, min(chunk, nb), len(xs), parts, len(adds), len(after)
        ),
        out_shape=outs,
        in_specs=[hspec()] * (len(xs) + 4 + len(flat) + len(after)),
        out_specs=(hspec(),) * len(parts),
        scratch_shapes=[pltpu.VMEM((nb * 512, WIDTH[p]), BF16) for p in parts]
        + [pltpu.VMEM(a.shape, a.dtype) for a in (*flat, *outs)]
        + [
            pltpu.VMEM((512, nb * 512), BF16),
            pltpu.SemaphoreType.DMA((nb, 2)),
            pltpu.SemaphoreType.DMA((nb, 4)),
            pltpu.SemaphoreType.DMA((max(1, len(flat)),)),
            pltpu.SemaphoreType.DMA((len(parts),)),
        ],
        compiler_params=params(),
        name="matmul_" + "_".join(parts),
    )(*xs, *weights, *flat, *after)


def down_kernel(
    x_hbm, here_hbm, far_hbm, cand_hbm, keep_hbm, give_hbm,
    x_ref, here_ref, far_ref, cand_ref, out_ref, sem,
):
    loads = fetch(
        ((x_hbm, x_ref), (here_hbm, here_ref), (cand_hbm, cand_ref), (far_hbm, far_ref)),
        sem,
    )
    settle(loads[:3])
    x = x_ref[...]
    cand = cand_ref[...].astype(F32)
    acc = None
    for a in range(0, 16, 2):
        if a == 8:
            settle(loads[3:])
        ref = here_ref if a < 8 else far_ref
        b = a % 8
        w = jnp.concatenate([ref[b], ref[b + 1]], axis=1)
        y = jnp.dot(x, w, preferred_element_type=F32)
        y = jnp.where(cand == float(a), y[:, :HEAD], jnp.where(cand == float(a + 1), y[:, HEAD:], 0.0))
        acc = y if acc is None else acc + y
    out_ref[...] = acc
    half = out_ref.shape[0] // 2
    core = lax.axis_index("tp").astype(I32) % 2
    mine = pl.ds(pl.multiple_of(core * half, half), half)
    other = pl.ds(pl.multiple_of((1 - core) * half, half), half)
    settle(fetch(((out_ref.at[mine], keep_hbm), (out_ref.at[other], give_hbm)), sem))


def down_product(x, here, far, cand):
    rows = x.shape[0]
    return pl.pallas_call(
        down_kernel,
        out_shape=(sds((rows // 2, HEAD), F32),) * 2,
        in_specs=[hspec()] * 4,
        out_specs=(hspec(), hspec()),
        scratch_shapes=[
            pltpu.VMEM(x.shape, BF16),
            pltpu.VMEM(here.shape, BF16),
            pltpu.VMEM(here.shape, BF16),
            pltpu.VMEM(cand.shape, BF16),
            pltpu.VMEM((rows, HEAD), F32),
            pltpu.SemaphoreType.DMA((4,)),
        ],
        compiler_params=params(),
        name="down_product",
    )(x, here, far, cand)


def turn_table():
    frequency = np.float32(THETA) ** (-(np.arange(HEAD // 2, dtype=np.float32) * 2.0 / HEAD))
    angles = np.arange(HEAD, dtype=np.float32)[:, None] * frequency.astype(np.float32)
    cos, sin = np.cos(angles.astype(np.float64)), np.sin(angles.astype(np.float64))
    rest = np.concatenate([cos, cos, -sin, sin], axis=1).astype(np.float32)
    terms = []
    for _ in range(3):
        terms.append(rest.astype(ml_dtypes.bfloat16))
        rest = rest - terms[-1].astype(np.float32)
    return np.concatenate(terms, axis=1)


def up_kernel(
    mine_hbm, other_hbm, far_hbm, cand_hbm, q_hbm, k_hbm, len_hbm, table_hbm, acc_hbm,
    out_hbm, kv_hbm, cos_hbm, sin_hbm,
    down_ref, far, cand_ref, q_here, k_here, len_ref, table_ref, acc_ref,
    out_ref, kv_ref, cos_ref, sin_ref, sem,
):
    half = mine_hbm.shape[0]
    core = lax.axis_index("tp").astype(I32) % 2
    mine = pl.ds(pl.multiple_of(core * half, half), half)
    other = pl.ds(pl.multiple_of((1 - core) * half, half), half)
    settle(
        fetch(
            (
                (mine_hbm, down_ref.at[mine]), (other_hbm, down_ref.at[other]),
                (far_hbm.at[:, 64:], far), (cand_hbm, cand_ref), (q_hbm, q_here),
                (k_hbm, k_here), (len_hbm, len_ref), (table_hbm, table_ref), (acc_hbm, acc_ref),
            ),
            sem,
        )
    )
    down = down_ref[...].astype(F32)
    cand = cand_ref[...].astype(F32)
    rows = down.shape[0]
    lane = iota((rows, HEAD), 1)
    upper = lane >= HEAD // 2
    other = pltpu.roll(down, HEAD // 2, 1)
    down_q = jnp.where(upper, other, down)
    down_k = jnp.where(upper, down, other)
    shift = jnp.where(upper, 1.0, 0.0)

    def spread(v):
        return jnp.concatenate(
            [jnp.where(cand == shift + float(2 * i), v, 0.0).astype(BF16) for i in range(8)], axis=1
        )

    sq, sk = spread(down_q), spread(down_k)
    q_all, k_all = q_here[...].reshape(512, 512), k_here[...].reshape(512, HEAD)

    def far_part(lo):
        return jnp.concatenate(
            [far[a, lo // 16 : lo // 16 + 4].reshape(64, HEAD) for a in range(8)], axis=0
        )

    w = [
        jnp.concatenate([q_all[:, h * HEAD : (h + 1) * HEAD], far_part(64 * h)], axis=0)
        for h in range(4)
    ]
    for h in (0, 2):
        at = slice(h * HEAD, (h + 2) * HEAD)
        out_ref[:, at] = acc_ref[:, at] + jnp.dot(
            sq, jnp.concatenate([w[h], w[h + 1]], axis=1), preferred_element_type=F32
        )
    kv_ref[...] = jnp.dot(
        sk, jnp.concatenate([k_all, far_part(256)], axis=0), preferred_element_type=F32
    )
    position = len_ref[...].astype(I32) + iota((rows, HEAD), 0) % 4
    pick = jnp.where(position == lane, 1.0, 0.0).astype(BF16)
    turns = jnp.dot(pick, table_ref[...], preferred_element_type=F32)
    turns = turns[:, :256] + turns[:, 256:512] + turns[:, 512:]
    cos_ref[...] = turns[:, :HEAD]
    sin_ref[...] = turns[:, HEAD:]
    settle(
        fetch(
            ((out_ref, out_hbm), (kv_ref, kv_hbm), (cos_ref, cos_hbm), (sin_ref, sin_hbm)), sem
        )
    )


def up_product(mine, other, far, cand, up_q, up_kv, length, acc):
    rows = cand.shape[0]
    ins = (cand, up_q, up_kv, length, jnp.asarray(turn_table()), acc)
    outs = (sds((rows, 512), F32),) + (sds((rows, HEAD), F32),) * 3
    return pl.pallas_call(
        up_kernel,
        out_shape=outs,
        in_specs=[hspec()] * 9,
        out_specs=(hspec(),) * 4,
        scratch_shapes=[pltpu.VMEM((rows, HEAD), BF16), pltpu.VMEM((8, 20, 16, HEAD), BF16)]
        + [pltpu.VMEM(a.shape, a.dtype) for a in ins + outs]
        + [pltpu.SemaphoreType.DMA((9,))],
        compiler_params=params(),
        name="up_product",
    )(mine, other, far, *ins)


GROUP = 4


def page_masks(mask_scr):
    for d in range(17):
        mask_scr[d] = jnp.where(iota((16, HEAD), 0) < d, 1.0, 0.0).astype(BF16)


def attend_kernel(
    meta_hbm, lens_hbm, own_hbm, far_hbm, rx_hbm, kv_hbm, kv2_hbm, cos_hbm, sin_hbm,
    pool_hbm, pool2_hbm, got_hbm, got2_hbm,
    out_hbm, new_hbm,
    meta_ref, lens_ref, own_ref, far_ref, rx_ref, kv_ref, kv2_ref, cos_ref, sin_ref, out_ref, new_ref,
    q_scr, f_scr, page_scr, mask_scr, sem,
):
    odd = lax.axis_index("tp").astype(I32) % 2
    def pages_from(i, pool, got):
        return [(pool, page_scr.at[i, :POOL])] + [
            (got.at[g, :64], page_scr.at[i, POOL + 64 * g : POOL + 64 * g + 64]) for g in range(8)
        ]

    copies = fetch(
        (
            (meta_hbm, meta_ref), (lens_hbm, lens_ref), *pages_from(0, pool_hbm, got_hbm),
            (far_hbm.at[:, 512:], far_ref), (rx_hbm, rx_ref), (kv_hbm, kv_ref), (kv2_hbm, kv2_ref),
            (cos_hbm, cos_ref), (sin_hbm, sin_ref), (own_hbm, own_ref),
            *pages_from(1, pool2_hbm, got2_hbm),
        ),
        sem,
    )
    page_masks(mask_scr)
    page_scr[0, ZERO_PAGE] = jnp.zeros((16, HEAD), BF16)
    settle(copies[:3])

    def keep(g, _):
        kept = []
        for e in range(4):
            for b in range(8):
                p = 4 * g + e
                kept.append((meta_ref[TARGET + b, p], page_scr[0, lens_ref[FROM + b, p]]))
        for at, page in kept:
            new_ref[at] = page
        return 0

    lax.fori_loop(0, 16, keep, 0)
    settle(copies[3:11])
    lax.fori_loop(16, 32, keep, 0)
    settle(copies[11:18])
    cos, sin = cos_ref[...], sin_ref[...]

    def turn(v):
        return v * cos + pltpu.roll(v, HEAD // 2, 1) * sin

    for h in range(4):
        at = slice(h * HEAD, (h + 1) * HEAD)
        q_scr[:, at] = turn(own_ref[:, at] + rx_ref[:, at])
    kv_own = far_ref[:, :HEAD] + rx_ref[:, 640:768] + kv_ref[...]
    kv_oth = far_ref[:, HEAD:] + rx_ref[:, 512:640] + kv2_ref[...]
    key = turn(jnp.where(odd == 0, kv_own, kv_oth))
    value = jnp.where(odd == 0, kv_oth, kv_own)
    f_scr[:, :HEAD] = key
    f_scr[:, HEAD : 2 * HEAD] = value
    f_scr[:, 2 * HEAD :] = jnp.where(odd == 0, key, value)

    gap = jnp.where(
        iota((256, 32), 0) // 32 == iota((256, 32), 1) // 4,
        iota((256, 32), 0) % 32 - iota((256, 32), 1) % 4,
        -1,
    )
    c32 = iota((1, 32), 1) // 4

    def edge_pages(g):
        at = [8 * g + e for e in range(8)]
        lengths = [lens_ref[LENGTH, p] for p in at]
        first = [jnp.minimum(n // 16, 6) for n in lengths]
        fresh = f_scr[pl.ds(pl.multiple_of(32 * g, 32), 32), 2 * HEAD :].astype(BF16)
        start = jnp.zeros((1, 32), I32)
        for e in range(8):
            start = jnp.where(c32 == e, lengths[e] - 16 * first[e], start)
        land = jnp.where(gap == start, 1.0, 0.0).astype(BF16)
        placed = jnp.dot(land, fresh, preferred_element_type=F32).astype(BF16)
        done = []
        for e, p in enumerate(at):
            for k in range(2):
                b = first[e] + k
                lo = e * 32 + k * 16
                page = page_scr[0, meta_ref[SOURCE + b, p]] * mask_scr[lens_ref[KEPT + b, p]]
                done.append((meta_ref[TARGET + b, p], page + placed[lo : lo + 16]))
        return done

    def edge(i, _):
        done = [pair for j in range(2) for pair in edge_pages(2 * i + j)]
        for to, page in done:
            new_ref[to] = page
        return 0

    scale = 1.0 / math.sqrt(HEAD)
    row2 = (iota((32, HEAD), 0) % 8) // 4
    lane32 = iota((32, HEAD), 1)
    col_a = jnp.where(row2 == 0, lane32, HEAD)
    col_b = jnp.where(row2 == 1, lane32, HEAD)
    row = iota((HEAD, HEAD), 0)
    col_new = iota((HEAD, HEAD), 1) - (row // 32) * 8 - (row % 8) // 4 * 4
    contract = (((1,), (1,)), ((), ()))

    def mixed_rows(g):
        q32 = q_scr[pl.ds(pl.multiple_of(32 * g, 32), 32), :]
        q = jnp.concatenate(
            [
                q32[8 * k : 8 * k + 8, h * HEAD : (h + 1) * HEAD]
                for k in range(GROUP)
                for h in range(4)
            ],
            axis=0,
        ).astype(BF16)
        block = pl.ds(pl.multiple_of((g // 4) * HEAD, HEAD), HEAD)
        fresh_k = f_scr[block, :HEAD].astype(BF16)
        fresh_v = f_scr[block, HEAD : 2 * HEAD].astype(BF16)
        new = lax.dot_general(q, fresh_k, contract, preferred_element_type=F32)
        rel = col_new - 32 * (g % 4)
        new = jnp.where((rel >= 0) & (rel <= row % 4), new, -1e30)
        lengths = [lens_ref[LENGTH, 8 * g + e] for e in range(8)]
        index = [meta_ref[SOURCE + b, 8 * g + e] for e in range(8) for b in range(8)]
        old_a, old_b = [], []
        for k in range(GROUP):
            keys = jnp.concatenate([page_scr[odd, j] for j in index[16 * k : 16 * k + 16]], axis=0)
            old = lax.dot_general(
                q[32 * k : 32 * k + 32], keys, contract, preferred_element_type=F32
            )
            old_a.append(jnp.where(col_a < lengths[2 * k], old[:, :HEAD], -1e30))
            old_b.append(jnp.where(col_b < lengths[2 * k + 1], old[:, HEAD:], -1e30))
        old_a, old_b = jnp.concatenate(old_a, axis=0), jnp.concatenate(old_b, axis=0)
        top = jnp.max(jnp.maximum(jnp.maximum(old_a, old_b), new), axis=1, keepdims=True)
        old_a, old_b, new = (jnp.exp((v - top) * scale) for v in (old_a, old_b, new))
        part = 1.0 / jnp.sum(old_a + old_b + new, axis=1, keepdims=True)
        old = jnp.concatenate([old_a * part, old_b * part], axis=1).astype(BF16)
        mixed = jnp.dot((new * part).astype(BF16), fresh_v, preferred_element_type=F32)
        old_mixed = []
        for k in range(GROUP):
            values = jnp.concatenate(
                [page_scr[1 - odd, j] for j in index[16 * k : 16 * k + 16]], axis=0
            )
            old_mixed.append(
                jnp.dot(old[32 * k : 32 * k + 32], values, preferred_element_type=F32)
            )
        mixed = (mixed + jnp.concatenate(old_mixed, axis=0)).astype(BF16)
        return mixed

    def mix(i, _):
        done = [mixed_rows(i * 4 + j) for j in range(4)]
        for j, mixed in enumerate(done):
            for n in range(2 * GROUP):
                slot = meta_ref[SLOT, (i * 4 + j) * 2 * GROUP + n]
                for h in range(4):
                    lo = n // 2 * 32 + h * 8 + n % 2 * 4
                    out_ref[slot, :, h * HEAD : (h + 1) * HEAD] = mixed[lo : lo + 4]
        return 0

    lax.fori_loop(0, 8, edge, 0)
    stores = fetch(((new_ref, new_hbm),), sem)
    settle(copies[18:])
    lax.fori_loop(0, 4, mix, 0)
    settle(stores + fetch(((out_ref, out_hbm),), sem, 1))


def attend(meta, lens, own, far, rx, kv, kv2, cos, sin, pool, pool2, got, got2):
    outs = (sds((128, 4, 512), BF16), sds(pool.shape, BF16))
    return pl.pallas_call(
        attend_kernel,
        out_shape=outs,
        in_specs=[hspec()] * 13,
        out_specs=(hspec(), hspec()),
        scratch_shapes=[pltpu.SMEM(meta.shape, I32), pltpu.SMEM(lens.shape, I32)]
        + [
            pltpu.VMEM(a.shape, a.dtype)
            for a in (own, sds((512, 256), F32), rx, kv, kv2, cos, sin, *outs)
        ]
        + [
            pltpu.VMEM((512, 512), F32),
            pltpu.VMEM((512, 3 * HEAD), F32),
            pltpu.VMEM((2, ZERO_PAGE + 1, 16, HEAD), BF16),
            pltpu.VMEM((17, 16, HEAD), BF16),
            pltpu.SemaphoreType.DMA((27,)),
        ],
        compiler_params=params(),
        name="attend",
    )(meta, lens, own, far, rx, kv, kv2, cos, sin, pool, pool2, got, got2)


def body(
    tokens,
    query_weight_matrix,
    key_value_weight,
    adapter_down_factors,
    adapter_up_query,
    adapter_up_key_value,
    storage_slot_adapter,
    slot_request_adapter,
    migration,
    lengths,
    previous_block_table,
    moved_block_table,
    paged_cache_pool,
):
    def other_core(a):
        return lax.ppermute(a, "tp", [(i, i ^ 1) for i in range(16)])

    def other_x(a):
        return lax.ppermute(a, "tp", [(i, i ^ 2) for i in range(16)])

    def along_y(a, d):
        return lax.ppermute(a, "tp", [(i, (i + 4 * d) % 16) for i in range(16)])

    def swap_rep(a):
        return lax.all_to_all(a, "rep", split_axis=0, concat_axis=0, tiled=True)

    send, own, cand, meta = plan(
        migration.reshape(8, 128), slot_request_adapter.reshape(8, 128),
        storage_slot_adapter.reshape(1, 64), lengths.reshape(1, 128),
        previous_block_table.T, moved_block_table.T, tokens,
    )
    packed, leaving = pack(
        meta, adapter_down_factors, adapter_up_query, adapter_up_key_value, paged_cache_pool
    )
    pool2 = other_core(paged_cache_pool)
    vq, vk = other_core(query_weight_matrix), other_core(key_value_weight)
    x, length, lens = join(own, swap_rep(send), meta, packed, pool2)
    far_down = swap_rep(packed)

    weights = (query_weight_matrix, key_value_weight, vq, vk)
    xh = other_x(x)
    yp = along_y(x, 1)
    ym = along_y(x, -1)
    full = (0, 512)
    ends = ((0, (0, 256), 0, 0), (1, (256, 512), 1, 0))
    yp2, ym2 = slices(ends, (256, 256), (yp, ym), (vq, vk))
    y2 = (along_y(yp2, 1), along_y(ym2, -1))

    keep, give = down_product(x, adapter_down_factors, far_down, cand)
    total = keep + other_core(give)
    total = total + other_x(total)
    leaving, total, _, _ = lax.optimization_barrier((leaving, total, xh, y2))
    got = swap_rep(leaving)

    xyp, xym = along_y(xh, 1), along_y(xh, -1)
    acc = matmul(
        ("far", "own"), ((0, 0), (3, 0), (1, 0), (2, 0)),
        (((0, *full),), ((1, *full),), ((2, *full),), ((3, 0, 256), (4, 0, 256))),
        (x, yp, ym, *y2), weights,
    )
    xyp2, xym2 = slices(ends, (256, 256), (xyp, xym), (acc[0],))
    xy2 = (along_y(xyp2, 1), along_y(xym2, -1))
    total = (total + along_y(total, 2)) + (along_y(total, 1) + along_y(total, -1))
    total = total.astype(BF16)
    other_total = other_core(total)
    acc_far, acc_own = matmul(
        ("far", "own"), ((0, 1), (3, 1), (1, 1), (2, 1)),
        (((0, *full),), ((1, *full),), ((2, *full),), ((3, 0, 256), (4, 0, 256))),
        (xh, xyp, xym, *xy2), weights, ((acc[0], acc[1]),), (other_total,),
    )
    rx = other_core(acc_far)
    got, acc_own = lax.optimization_barrier((got, acc_own))
    own, kv, cos, sin = up_product(
        total, other_total, got, cand, adapter_up_query, adapter_up_key_value, length, acc_own
    )
    return attend(
        meta, lens, own, acc_far, rx, kv, other_core(kv), cos, sin,
        paged_cache_pool, pool2, got, other_core(got),
    )


def solution(mesh):
    in_specs = (
        P("rep", None, "tp"),
        P(None, "tp"),
        P(None, "tp"),
        P("rep", "tp", None),
        P("rep", None, "tp"),
        P("rep", None, "tp"),
        P(),
        P(),
        P(),
        P("rep"),
        P("rep", None),
        P("rep", None),
        P("rep", None, "tp"),
    )
    out_specs = (P("rep", None, "tp"), P("rep", None, "tp"))
    return jax.shard_map(body, mesh=mesh, in_specs=in_specs, out_specs=out_specs, check_vma=False)
```
